32 devices in a mesh: member: 2 (over x), band: 16 (over z, y, core).
Axes of the slice: x: 2, y: 2, z: 4, core: 2. Of those that a mesh axis runs over, the one named last changes fastest.
Arguments:
- state: float32 [14, 6, 2048, 1024], P('member', None, 'band'), parts along dimension 0, may hold values from -6 to 6
- courant_lon: float32 [4096, 1024], P(('member', 'band')), parts along dimension 0, may hold values from 0.05 to 0.45
- courant_lat: float32 [4096, 1024], P(('member', 'band')), parts along dimension 0, may hold values from 0.05 to 0.45
- reference_field: float32 [12, 2048, 1024], P('member', 'band'), parts along dimension 0, may hold values from -6 to 6
- nudge_rate: float32 [512], replicated, may hold values from 0.05 to 1
Outputs:
- new_state: float32 [14, 6, 2048, 1024], P('member', None, 'band'), parts along dimension 0
The draws below stay inside these ranges and needn't reach their ends.
There are 2 independent parts, one for each index of `member`. The reference program is written for one: setup_inputs(seed, part) draws one part's arguments, and reference() takes and returns one part's arrays. A program takes and returns all parts, laid end to end along the dimension named above; an argument that names none is the same for every part. Nothing has to cross between parts.
All inputs are finite; a program needn't handle non-finite values.
Results may differ from the reference program's by a relative error of at most 0.0003.
Values sent between devices are 32-bit elements; how exact they have to be, the bound alone decides.
No kernel may reach another device: no remote copies, remote signals or barrier semaphores. Data moves between devices by JAX's collectives and lax.ppermute only.
A program may use at most 256 MiB of HBM per device.

```python
import math
import jax
import jax.numpy as jnp
from jax import lax

NLON = 2048
NLAT = 1024
MW = 512
FIELDS = 7
LEV = 6
STEPS = 2


def levels(key, extent, shards, least, high):
    gain, own = 1.0, jax.random.fold_in(key, 6)
    for dim, parts in shards:
        draws = jnp.exp(jax.random.uniform(jax.random.fold_in(own, dim), (parts,), jnp.float32, least / len(shards), high / len(shards)))
        gain = gain * jnp.repeat(draws, extent[dim] // parts).reshape([-1 if axis == dim else 1 for axis in range(len(extent))])
    return gain


def noise(stream_key, extent, spread, reach, cuts=(), dtype=jnp.bfloat16):
    values = jax.random.normal(stream_key, extent, jnp.float32) * spread
    if len(cuts) > 0:
        values = levels(stream_key, extent, cuts, -0.22, 0.18) * values
    return jnp.clip(values, min=-reach, max=reach).astype(dtype)


def setup_inputs(seed: int = 0, part: int = 0) -> dict:
    arg_keys = jax.random.split(jax.random.key(seed), 6)
    own_keys = jax.random.split(jax.random.fold_in(arg_keys[5], part), 6)
    return {
        "state": noise(own_keys[0], (FIELDS, LEV, NLON, NLAT), 1.0, 6.0, ((2, 16),), jnp.float32),
        "courant_lon": jnp.clip(0.05 + 0.39999999 * jax.random.uniform(own_keys[1], (NLON, NLAT), jnp.float32) ** levels(own_keys[1], (NLON, NLAT), ((0, 16),), -0.2, 0.2), 0.05, 0.45),
        "courant_lat": jnp.clip(0.05 + 0.39999999 * jax.random.uniform(own_keys[2], (NLON, NLAT), jnp.float32) ** levels(own_keys[2], (NLON, NLAT), ((0, 16),), -0.2, 0.2), 0.05, 0.45),
        "reference_field": noise(own_keys[3], (LEV, NLON, NLAT), 1.0, 6.0, ((1, 16),), jnp.float32),
        "nudge_rate": jnp.clip(jnp.exp(jax.random.uniform(arg_keys[4], (MW,), jnp.float32, math.log(0.05), math.log(1.0))), 0.05, 1.0),
    }


highest = lax.Precision.HIGHEST

def latitude_terms(lat_total):
    centres = (jnp.arange(lat_total).astype(jnp.float32) + 0.5) * (math.pi / lat_total)
    return (jnp.cos(centres), jnp.log(jnp.sin(centres)), jnp.sin(centres) * (math.pi / lat_total))

def norm_table(wave_total):
    orders = jnp.arange(1, wave_total).astype(jnp.float32)
    terms = jnp.log((2.0 * orders + 1.0) / (2.0 * orders))
    return jnp.concatenate([jnp.zeros((1,), jnp.float32), jnp.cumsum(terms)])

def start_value(wave_ids, log_sin, norms):
    matches = wave_ids[:, None] == jnp.arange(norms.shape[0]).astype(jnp.int32)[None, :]
    log_norm = lax.optimization_barrier(jnp.sum(jnp.where(matches, norms[None, :], 0.0), axis=1))
    orders = wave_ids.astype(jnp.float32)
    return 0.5 * log_norm[:, None] + orders[:, None] * log_sin[None, :] - 0.5 * math.log(2.0)

def legendre_table(wave_rows, offset_rows, upper_rows, starts, cosines):

    def advance(carry, inputs):
        earlier, latest, deficit = carry
        wave_now, offset_now, upper_now = inputs
        orders = wave_now.astype(jnp.float32)[:, None]
        degree = (wave_now + offset_now).astype(jnp.float32)[:, None]
        factor_now = jnp.sqrt((4.0 * degree * degree - 1.0) / jnp.maximum(degree * degree - orders * orders, 1.0))
        below = degree - 1.0
        older_sq = jnp.where(offset_now[:, None] >= 2, (4.0 * below * below - 1.0) / jnp.maximum(below * below - orders * orders, 1.0), 1.0)
        factor_old = jnp.where(offset_now[:, None] >= 2, factor_now / jnp.sqrt(older_sq), 0.0)
        log_start = jnp.where(upper_now[:, None] == 1, starts[:, 1], starts[:, 0])
        clamped = jnp.maximum(log_start, -80.0)
        fresh = offset_now[:, None] == 0
        recurred = factor_now * cosines[None, :] * latest - factor_old * earlier
        largest = jnp.maximum(jnp.abs(recurred), jnp.abs(latest))
        absorb = jnp.maximum(deficit, -jnp.log(jnp.maximum(largest, 1.0)))
        rescale = jnp.exp(absorb)
        next_latest = jnp.where(fresh, jnp.exp(clamped), recurred * rescale)
        next_earlier = jnp.where(fresh, jnp.zeros_like(latest), latest * rescale)
        next_deficit = jnp.where(fresh, log_start - clamped, deficit - absorb)
        result_row = next_latest * jnp.exp(next_deficit)
        return ((next_earlier, next_latest, next_deficit), result_row)
    zero_row = jnp.zeros_like(starts[:, 0])
    final_carry, rows = lax.scan(advance, (zero_row, zero_row, zero_row), (wave_rows.T, offset_rows.T, upper_rows.T), unroll=16)
    return jnp.transpose(rows, (1, 0, 2))

def reference(state, courant_lon, courant_lat, reference_field, nudge_rate):
    advected = state
    for turn_index in range(STEPS):
        west_cells = jnp.roll(advected, 1, axis=2)
        south_cells = jnp.concatenate([jnp.zeros_like(advected[:, :, :, :1]), advected[:, :, :, :-1]], axis=3)
        advected = advected - courant_lon * (advected - west_cells) - courant_lat * (advected - south_cells)
    anomaly = reference_field - advected[0]
    spectrum = jnp.fft.rfft(anomaly, axis=1)[:, :MW] / NLON
    cosines, log_sin, quad_weights = latitude_terms(NLAT)
    norms = norm_table(MW)
    fourier = jnp.stack([jnp.real(spectrum), jnp.imag(spectrum)], axis=0)
    weighted = jnp.transpose(fourier, (2, 0, 1, 3)) * quad_weights
    group_size = 8
    grouped = weighted.reshape(MW // group_size, group_size, 2, LEV, NLAT)
    rate_padded = jnp.concatenate([nudge_rate, jnp.zeros((MW,), jnp.float32)])

    def one_group(inputs):
        wave_block, group_index = inputs
        wave_ids = group_index * group_size + jnp.arange(group_size).astype(jnp.int32)
        offsets = jnp.arange(MW).astype(jnp.int32)
        wave_rows = jnp.broadcast_to(wave_ids[:, None], (group_size, MW))
        offset_rows = jnp.broadcast_to(offsets[None, :], (group_size, MW))
        initial = start_value(wave_ids, log_sin, norms)
        legendre = legendre_table(wave_rows, offset_rows, jnp.zeros_like(wave_rows), jnp.stack([initial, initial], 1), cosines)
        degrees = wave_rows + offset_rows
        rate_rows = jnp.where(degrees < MW, jnp.take(rate_padded, degrees), 0.0)
        analysed = jnp.einsum('skj,sclj->skcl', legendre, wave_block, precision=highest)
        scaled = analysed * rate_rows[:, :, None, None]
        return jnp.einsum('skj,skcl->sclj', legendre, scaled, precision=highest)
    synthesised = lax.map(one_group, (grouped, jnp.arange(MW // group_size).astype(jnp.int32)))
    synthesised = synthesised.reshape(MW, 2, LEV, NLAT)
    pieces = jnp.transpose(synthesised, (1, 2, 0, 3))
    complex_spec = pieces[0] + 1j * pieces[1]
    padded = jnp.pad(complex_spec, ((0, 0), (0, NLON // 2 + 1 - MW), (0, 0)))
    increment = jnp.fft.irfft(padded, n=NLON, axis=1) * NLON
    nudged = advected[0] + increment
    return jnp.concatenate([nudged[None], advected[1:]], axis=0)
```

```python
import functools
import math

import jax
import jax.numpy as jnp
import ml_dtypes
import numpy as np
from jax import lax
from jax.experimental import pallas as pl
from jax.experimental.pallas import tpu as pltpu
from jax.sharding import PartitionSpec as P

STEPS = 2
GROUP = 8
STRIPS = 16
UNIT = 2
ROWS = 64
QUADS = ROWS // 32
SHIFT = 100
DROP = 120
TOP = 20
CHUNKS = 4
F32 = jnp.float32
BF16 = jnp.bfloat16


def split_np(values):
    high = values.astype(ml_dtypes.bfloat16)
    low = (values - high.astype(np.float64)).astype(ml_dtypes.bfloat16)
    return high, low


def split(values):
    high = values.astype(BF16)
    return high, (values - high.astype(F32)).astype(BF16)


def dot(left, right):
    return jnp.dot(left, right, preferred_element_type=F32)


class Layout:
    def __init__(self, wave_total, lat_total, lon_total, band_count):
        self.waves, self.lats, self.lons, self.band = wave_total, lat_total, lon_total, band_count
        self.half = lat_total // 2
        self.groups = wave_total // (2 * GROUP)
        self.blocks = [-(-(wave_total - 2 * GROUP * t) // ROWS) for t in range(self.groups)]
        shares = [0] * CHUNKS
        self.chunks = [[] for _ in range(CHUNKS)]
        for t in sorted(range(self.groups), key=lambda t: -self.blocks[t]):
            q = int(np.argmin(shares))
            self.chunks[q].append(t)
            shares[q] += self.blocks[t]
        self.chunks = [chunk for chunk in self.chunks if chunk]
        self.order = [t for chunk in self.chunks for t in chunk]
        ends = np.cumsum([0] + [2 * GROUP * len(chunk) for chunk in self.chunks])
        self.cuts = [(int(b), int(e)) for b, e in zip(ends[:-1], ends[1:])]

    def wave_ids(self, core):
        ids = []
        for t in self.order:
            ids.append(GROUP * (2 * t + core) + np.arange(GROUP))
        return np.stack(ids)

    def items(self, chunk):
        items = [(local, b) for local, t in enumerate(chunk) for b in range(self.blocks[t])]
        while len(items) % (2 * UNIT):
            items.append((len(chunk) - 1, -1))
        return items

    @functools.cached_property
    def angles(self):
        return math.pi * (np.arange(self.half) + 0.5) / self.lats

    @functools.cached_property
    def recurrence(self):
        depth = self.waves + 2 * ROWS
        m = np.arange(self.waves, dtype=np.float64)[:, None]
        k = np.arange(depth, dtype=np.float64)[None, :]
        n = m + k
        a = np.ones((self.waves, depth))
        a[:, 1:] = np.sqrt((4 * n * n - 1)[:, 1:] / (n * n - m * m)[:, 1:])
        c = np.ones_like(a)
        c[:, 1] = a[:, 1]
        for i in range(2, depth):
            c[:, i] = a[:, i] / a[:, i - 1] * c[:, i - 2]
        alpha = np.zeros_like(a)
        alpha[:, 1:] = a[:, 1:] * c[:, :-1] / c[:, 1:]
        return alpha, c

    @functools.cached_property
    def starts(self):
        orders = np.arange(1, self.waves)
        norms = np.concatenate([[0.0], np.cumsum(np.log((2.0 * orders + 1) / (2.0 * orders)))])
        m = np.arange(self.waves)[:, None]
        logs = 0.5 * norms[:, None] + m * np.log(np.sin(self.angles))[None, :] - 0.5 * math.log(2.0)
        exps = logs / math.log(2.0) + SHIFT
        deficit = np.where(exps < -SHIFT, np.ceil((-SHIFT - exps) / DROP), 0.0)
        return np.exp2(exps + DROP * deficit), deficit

    def tables(self, chunk):
        alpha, c = self.recurrence
        mant, deficit = self.starts
        items = self.items(chunk)
        out_alpha = np.zeros((2, len(items), GROUP, 128), np.float32)
        out_c = np.zeros((2, len(items), ROWS, 128), np.float32)
        shape = (2, len(chunk) * GROUP, self.half)
        out_start, out_deficit = np.zeros(shape, np.float32), np.zeros(shape, np.float32)
        rows = np.concatenate([np.arange(0, ROWS, 2), np.arange(1, ROWS, 2)])
        for core in range(2):
            for local, t in enumerate(chunk):
                waves = GROUP * (2 * t + core) + np.arange(GROUP)
                place = slice(GROUP * local, GROUP * (local + 1))
                out_start[core, place], out_deficit[core, place] = -mant[waves], deficit[waves]
            for i, (local, b) in enumerate(items):
                if b < 0:
                    continue
                waves = GROUP * (2 * chunk[local] + core) + np.arange(GROUP)
                out_alpha[core, i, :, :ROWS] = alpha[waves, ROWS * b : ROWS * (b + 1)]
                squares = c[waves][:, ROWS * b + rows] ** 2 * 2.0**-SHIFT
                out_c[core, i] = np.tile(squares.T, (1, 128 // GROUP))
        return out_alpha, out_start, out_deficit, out_c

    def fourier_tables(self):
        local = self.lons // self.band
        forward = np.zeros((self.band, self.waves, 2 * local))
        inverse = np.zeros((self.band, 2 * local, self.waves))
        for place in range(self.band):
            waves = self.wave_ids(place % 2)
            lons = np.concatenate([local * place + np.arange(local), local * (place ^ 1) + np.arange(local)])
            phase = (waves[:, :, None] * lons % self.lons) * (2 * math.pi / self.lons)
            both = np.stack([np.cos(phase), -np.sin(phase)], axis=1).reshape(self.waves, 2 * local)
            double = np.where(waves == 0, 1.0, 2.0)
            double = np.stack([double, double], axis=1).reshape(self.waves)
            forward[place] = both / self.lons
            inverse[place] = (both * double[:, None]).T
        return [np.concatenate(split_np(t), axis=1) for t in (forward, inverse)]


def south_of(cells, lane_ids):
    return jnp.where(lane_ids == 0, 0.0, pltpu.roll(cells, 1, 1))


def two_steps(cells, edge, lon, lat, lon_edge, lat_edge, store):
    shape = (8, cells.shape[1])
    row_ids = lax.broadcasted_iota(jnp.int32, shape, 0)
    lane_ids = lax.broadcasted_iota(jnp.int32, shape, 1)
    outer = jnp.broadcast_to(edge[0:1], shape)
    inner = jnp.broadcast_to(edge[1:2], shape)
    inner_once = (
        inner - lon_edge * (inner - outer) - lat_edge * (inner - south_of(inner, lane_ids))
    )

    def strip(i, carry):
        before, before_once = carry
        rows = pl.ds(pl.multiple_of(8 * i, 8), 8)
        now, east, north = cells[rows, :], lon[rows, :], lat[rows, :]
        turned = pltpu.roll(now, 1, 0)
        west = jnp.where(row_ids == 0, before, turned)
        once = now - east * (now - west) - north * (now - south_of(now, lane_ids))
        turned_once = pltpu.roll(once, 1, 0)
        west = jnp.where(row_ids == 0, before_once, turned_once)
        store(rows, once - east * (once - west) - north * (once - south_of(once, lane_ids)))
        return turned, turned_once

    lax.fori_loop(0, cells.shape[0] // 8, strip, (inner, inner_once), unroll=STRIPS)


def reversed_lanes(values, flip):
    width = flip.shape[0]
    high, rest = split(values)
    mid = rest
    low = (values - high.astype(F32) - mid.astype(F32)).astype(BF16)
    pieces = []
    for at in range(values.shape[1] // width - 1, -1, -1):
        cut = slice(at * width, (at + 1) * width)
        pieces.append(dot(high[:, cut], flip) + (dot(mid[:, cut], flip) + dot(low[:, cut], flip)))
    return jnp.concatenate(pieces, axis=1)


def first_field_kernel(cells, edge, lon, lat, courant_edge, target, flip, moved, folded):
    def store(rows, values):
        moved[0, rows, :] = values

    two_steps(
        cells.at[0, 0], edge[0], lon, lat, courant_edge[0:1], courant_edge[1:2], store
    )
    anomaly = target[0] - moved[0]
    half = anomaly.shape[1] // 2
    north = anomaly[:, :half]
    south = reversed_lanes(anomaly[:, half:], flip[...])
    folded[0, :, :half] = north + south
    folded[0, :, half:] = north - south


def other_fields_kernel(cells, edge, lon, lat, courant_edge, moved):
    def store(rows, values):
        moved[0, 0, rows, :] = values

    two_steps(
        cells.at[0, 0], edge[0], lon, lat, courant_edge[0:1], courant_edge[1:2], store
    )


def finish_kernel(flip, moved, mine, theirs, whole, out):
    del whole
    total = mine[0, 0] + theirs[0]
    half = total.shape[1] // 2
    even, odd = total[:, :half], total[:, half:]
    out[0, 0, :, :half] = moved[0, :, :half] + (even + odd)
    out[0, 0, :, half:] = moved[0, :, half:] + reversed_lanes(even - odd, flip[...])


def forward_kernel(cuts, place, table, mine, theirs, quad, *outs):
    del place
    a_high, a_low = split(jnp.concatenate([mine[0], theirs[0]], axis=0))
    waves = table.shape[1] // 2
    wide = dot(table[0], a_high)
    total = (wide[:waves] + (wide[waves:] + dot(table[0, :waves], a_low))) * quad[...]
    for out, (begin, end) in zip(outs, cuts):
        out[0] = total[begin:end]


def inverse_kernel(place, table, *refs):
    del place
    out = refs[-1]
    s_high, s_low = split(jnp.concatenate([ref[0] for ref in refs[:-1]], axis=0))
    lons = table.shape[1] // 2
    wide = dot(table[0], s_high)
    total = wide[:lons] + (wide[lons:] + dot(table[0, :lons], s_low))
    out[0, 0], out[1, 0] = total[: lons // 2], total[lons // 2 :]


def table_block(index, first, local, carry, alpha, start, deficit, mu, scaled, even, odd):
    earlier, latest, owed = carry
    count = len(earlier)
    fresh = first == 1
    rows = pl.ds(pl.multiple_of(local * GROUP, GROUP), GROUP)
    factors = alpha[0, index]
    earlier, latest, owed = list(earlier), list(latest), list(owed)
    for b in range(count):
        lanes = slice(128 * b, 128 * (b + 1))
        earlier[b] = jnp.where(fresh, start[0, rows, lanes], earlier[b])
        latest[b] = jnp.where(fresh, 0.0, latest[b])
        if scaled[b]:
            owed[b] = jnp.where(fresh, deficit[0, rows, lanes], owed[b])
    values = [[None] * ROWS for _ in range(count)]
    for segment in range(0, ROWS, 16):
        for b in range(count):
            if scaled[b]:
                large = jnp.maximum(jnp.abs(earlier[b]), jnp.abs(latest[b])) > 2.0**TOP
                down = jnp.logical_and(large, owed[b] > 0.0)
                factor = jnp.where(down, 2.0**-DROP, 1.0)
                earlier[b] = earlier[b] * factor
                latest[b] = latest[b] * factor
                owed[b] = owed[b] - jnp.where(down, 1.0, 0.0)
        for k in range(segment, segment + 16):
            spread = jnp.broadcast_to(factors[:, k : k + 1], (GROUP, 128))
            for b in range(count):
                fresh_value = (spread * mu[:, 128 * b : 128 * (b + 1)]) * latest[b] - earlier[b]
                earlier[b], latest[b] = latest[b], fresh_value
                values[b][k] = fresh_value
        for b in range(count):
            lanes = slice(128 * b, 128 * (b + 1))
            for k in range(segment, segment + 16, 4):
                for parity, store in ((0, even), (1, odd)):
                    pair = jnp.concatenate(
                        [values[b][k + parity], values[b][k + parity + 2]], axis=0
                    )
                    if scaled[b]:
                        keep = jnp.concatenate([owed[b], owed[b]], axis=0) == 0.0
                        pair = jnp.where(keep, pair, 0.0)
                    high, low = split(pair)
                    at = 4 * k
                    store[at : at + 16, lanes] = high
                    store[4 * ROWS + at : 4 * ROWS + at + 16, lanes] = low
    return tuple(earlier), tuple(latest), tuple(owed)


def own_lane_mask(value):
    wave = lax.broadcasted_iota(jnp.int32, (GROUP, 128), 0)
    lane = lax.broadcasted_iota(jnp.int32, (GROUP, 128), 1)
    return jnp.where(lane % GROUP == wave, value, 0.0)


def run_blocks(count, tables, use, lat_blocks, scaled, buffers):
    firsts, locals_, alpha, start, deficit, mu = tables
    ahead, behind = buffers
    angles = jnp.broadcast_to(mu[...], (GROUP, mu.shape[1]))
    zero = jnp.zeros((GROUP, 128), F32)
    carry = tuple(tuple(zero for _ in range(lat_blocks)) for _ in range(3))

    def stage(base, carry, made, used):
        use([jnp.maximum(base - UNIT + j, j) for j in range(UNIT)], used)
        for j in range(UNIT):
            i = base + j
            carry = table_block(
                i, firsts[i], locals_[i], carry, alpha, start, deficit, angles, scaled, *made[j]
            )
        return carry

    def two(step, carry):
        carry = stage(2 * UNIT * step, carry, ahead, behind)
        return stage(2 * UNIT * step + UNIT, carry, behind, ahead)

    lax.fori_loop(0, count // (2 * UNIT), two, carry)
    use([jnp.int32(count - UNIT + j) for j in range(UNIT)], behind)


def buffer_pairs(refs):
    pairs = [(refs[2 * j], refs[2 * j + 1]) for j in range(2 * UNIT)]
    return pairs[:UNIT], pairs[UNIT:]


def clear(pairs):
    for pair in pairs:
        for ref in pair:
            ref[...] = jnp.zeros_like(ref)


def slot_of(item, count, owned):
    quarter = item // (count // 4)
    return quarter ^ owned, (item - quarter * (count // 4)) * 24 * QUADS


def analysis_kernel(
    count,
    levels,
    scaled,
    where,
    firsts,
    locals_,
    alpha,
    start,
    deficit,
    mu,
    waves,
    out,
    weights,
    *refs,
):
    buffers = buffer_pairs(refs)
    groups = waves.shape[1] // (2 * GROUP)
    half = waves.shape[2] // 2
    columns = levels * 2 * GROUP

    def prepare(group, _):
        rows = pl.ds(pl.multiple_of(group * 2 * GROUP, 2 * GROUP), 2 * GROUP)
        for parity in range(2):
            block = waves[:, rows, parity * half : (parity + 1) * half].reshape(columns, half)
            block = jnp.concatenate([block, jnp.zeros((128 - columns, half), F32)], axis=0)
            high, low = split(block.T)
            weights[group, parity, :, 0:128] = high
            weights[group, parity, :, 128:256] = low
        return 0

    lax.fori_loop(0, groups, prepare, 0)
    clear(buffers[1])
    owned = where[1]
    mask = own_lane_mask(2.0**-SHIFT)
    lane = lax.broadcasted_iota(jnp.int32, (GROUP, 128), 1)
    table = 4 * ROWS

    def use(items, stores):
        products = []
        for item, pair in zip(items, stores):
            group = locals_[item]
            products.append([dot(pair[p][...], weights[group, p]) for p in range(2)])
        for item, pair in zip(items, products):
            sums = []
            for both in pair:
                product = both[:table, 0:128] + (both[:table, 128:256] + both[table:, 0:128])
                picked = product.reshape(table // GROUP, GROUP, 128) * mask[None]
                sums.append(jnp.sum(picked, axis=1))
            slot, at = slot_of(item, count, owned)
            for quad in range(QUADS):
                tiles = []
                for j in range(4 * quad, 4 * quad + 4):
                    parity, row = divmod(8 * j, ROWS // 2)
                    tiles.append(sums[parity][row : row + 8])
                second, third = pltpu.roll(tiles[1], 96, 1), pltpu.roll(tiles[2], 64, 1)
                packed = (
                    jnp.where(lane < 96, tiles[0], second),
                    jnp.where(lane < 64, second, third),
                    jnp.where(lane < 32, third, pltpu.roll(tiles[3], 32, 1)),
                )
                for j in range(3):
                    rows = pl.ds(pl.multiple_of(at + 24 * quad + 8 * j, 8), 8)
                    out[slot, rows, :] = packed[j]

    run_blocks(
        count,
        (firsts, locals_, alpha, start, deficit, mu),
        use,
        half // 128,
        scaled,
        buffers,
    )


def synthesis_kernel(
    count,
    levels,
    scaled,
    where,
    firsts,
    locals_,
    degrees,
    alpha,
    start,
    deficit,
    mu,
    squares,
    rates,
    coeffs,
    out,
    *refs,
):
    buffers = buffer_pairs(refs)
    half = mu.shape[1]
    columns = levels * 2 * GROUP
    clear(buffers[1])
    owned = where[1]
    mask = own_lane_mask(1.0)
    lane = lax.broadcasted_iota(jnp.int32, (GROUP, 128), 1)
    table = 4 * ROWS

    def use(items, stores):
        totals = []
        for item, pair in zip(items, stores):
            slot, at = slot_of(item, count, owned)
            tiles = []
            for quad in range(QUADS):
                packed = []
                for j in range(3):
                    rows = pl.ds(pl.multiple_of(at + 24 * quad + 8 * j, 8), 8)
                    packed.append(coeffs[slot, rows, :])
                tiles += [
                    packed[0],
                    pltpu.roll(jnp.where(lane < 64, packed[1], packed[0]), 32, 1),
                    pltpu.roll(jnp.where(lane < 32, packed[2], packed[1]), 64, 1),
                    pltpu.roll(packed[2], 96, 1),
                ]
            degree_rows = pl.ds(pl.multiple_of(degrees[item], 8), ROWS // 2)
            share = ROWS // 2
            for parity in range(2):
                parts = tiles[parity * 2 * QUADS : (parity + 1) * 2 * QUADS]
                scale = squares[0, item, share * parity : share * (parity + 1)]
                block = jnp.concatenate(parts, axis=0) * (scale * rates[parity, degree_rows])
                wide = jnp.broadcast_to(block[:, None, :], (share, GROUP, 128)) * mask[None]
                high, low = split(wide.reshape(table, 128).T[:columns])
                left = jnp.concatenate(
                    [
                        jnp.concatenate([high, high], axis=1),
                        jnp.concatenate([low, jnp.zeros_like(low)], axis=1),
                    ],
                    axis=0,
                )
                total = dot(left, pair[parity][...])
                totals.append(total[:columns] + total[columns:])
        for j, item in enumerate(items):
            target = pl.ds(pl.multiple_of(locals_[item] * 2 * GROUP, 2 * GROUP), 2 * GROUP)
            for parity in range(2):
                lanes = slice(parity * half, (parity + 1) * half)
                before = jnp.where(firsts[item] == 1, 0.0, out[:, target, lanes])
                total = totals[2 * j + parity].reshape(levels, 2 * GROUP, half)
                out[:, target, lanes] = before + total

    run_blocks(
        count,
        (firsts, locals_, alpha, start, deficit, mu),
        use,
        half // 128,
        scaled,
        buffers,
    )


def chip_sum(slots, band_count):
    chips = band_count // 2
    steps = [1 << b for b in range(chips.bit_length() - 1)]
    part = slots[:2] + (yield slots[2:], steps[0])
    part = part[:1] + (yield part[1:], steps[1])
    for step in steps[2:]:
        part = part + (yield part, step)
    part = jnp.concatenate([part, (yield part, steps[1])], axis=0)
    return jnp.concatenate([part, (yield part, steps[0])], axis=0)


def chip_move(value, step, band_count):
    ends = []
    for c in range(band_count // 2):
        ends += [(2 * c, 2 * (c ^ step)), (2 * c + 1, 2 * (c ^ step) + 1)]
    return lax.ppermute(value, "band", ends)


class Pipeline:
    def __init__(self, band_count):
        self.band_count = band_count
        self.active = {}
        self.done = {}

    def begin(self, key, slots):
        steps = chip_sum(slots, self.band_count)
        self.active[key] = [steps, next(steps)]

    def compute(self, operands, call):
        keys = list(self.active)
        payloads = [self.active[k][1][0] for k in keys]
        operands, payloads = lax.optimization_barrier((tuple(operands), payloads))
        arrived = [
            chip_move(p, self.active[k][1][1], self.band_count) for k, p in zip(keys, payloads)
        ]
        result, arrived = lax.optimization_barrier((call(*operands), arrived))
        for k, value in zip(keys, arrived):
            entry = self.active[k]
            try:
                entry[1] = entry[0].send(value)
            except StopIteration as stop:
                self.done[k] = stop.value
                del self.active[k]
        return result


def full(shape):
    return pl.BlockSpec(shape, lambda *_: (0,) * len(shape))


def cost(micros):
    return pl.CostEstimate(flops=int(micros * 1e9), bytes_accessed=1 << 20, transcendentals=0)


def params(limit=56):
    return pltpu.CompilerParams(vmem_limit_bytes=limit << 20)


def body(state, courant_lon, courant_lat, reference_field, nudge_rate):
    fields, levels, lon_local, lat_total = state.shape
    band_count = lax.axis_size("band")
    place = lax.axis_index("band")
    wave_total = nudge_rate.shape[0]
    lay = Layout(wave_total, lat_total, lon_local * band_count, band_count)
    half = lay.half
    plane = (lon_local, lat_total)
    chip = place // 2
    owned = 2 * (chip % 2) + (chip // 2) % 2
    where = jnp.stack([place % 2, owned, place]).astype(jnp.int32)

    east = [(i, (i + 1) % band_count) for i in range(band_count)]
    peer = [(i, i ^ 1) for i in range(band_count)]
    edge_rows = jnp.concatenate(
        [
            state[0, :, lon_local - STEPS :, :].reshape(levels * STEPS, lat_total),
            courant_lon[lon_local - 1 :],
            courant_lat[lon_local - 1 :],
        ],
        axis=0,
    )
    arrived = lax.ppermute(edge_rows, "band", east)
    first_edge = arrived[: levels * STEPS].reshape(levels, STEPS, lat_total)
    courant_edge = arrived[levels * STEPS :]
    flip_width = min(256, half)
    flip = jnp.asarray(np.eye(flip_width)[::-1].astype(ml_dtypes.bfloat16))

    moved, folded = pl.pallas_call(
        first_field_kernel,
        grid=(levels,),
        in_specs=[
            pl.BlockSpec((1, 1) + plane, lambda l: (0, l, 0, 0)),
            pl.BlockSpec((1, STEPS, lat_total), lambda l: (l, 0, 0)),
            full(plane),
            full(plane),
            full((2, lat_total)),
            pl.BlockSpec((1,) + plane, lambda l: (l, 0, 0)),
            full((flip_width, flip_width)),
        ],
        out_specs=[pl.BlockSpec((1,) + plane, lambda l: (l, 0, 0))] * 2,
        out_shape=[jax.ShapeDtypeStruct((levels,) + plane, F32)] * 2,
        compiler_params=params(),
        name="first_field",
    )(state, first_edge, courant_lon, courant_lat, courant_edge, reference_field, flip)
    peer_folded = lax.ppermute(folded, "band", peer)

    other_rows = state[1:, :, lon_local - STEPS :, :].reshape((fields - 1) * levels, STEPS, lat_total)
    other_edge = lax.ppermute(other_rows, "band", east)

    def others_call(state, other_edge, courant_lon, courant_lat, courant_edge):
        return pl.pallas_call(
            other_fields_kernel,
            grid=((fields - 1) * levels,),
            in_specs=[
                pl.BlockSpec((1, 1) + plane, lambda i: (1 + i // levels, i % levels, 0, 0)),
                pl.BlockSpec((1, STEPS, lat_total), lambda i: (i, 0, 0)),
                full(plane),
                full(plane),
                full((2, lat_total)),
            ],
            out_specs=pl.BlockSpec((1, 1) + plane, lambda i: (1 + i // levels, i % levels, 0, 0)),
            out_shape=jax.ShapeDtypeStruct(state.shape, F32),
            compiler_params=params(),
            cost_estimate=cost(14.0),
            name="other_fields",
        )(state, other_edge, courant_lon, courant_lat, courant_edge)

    forward, inverse = [jnp.asarray(t) for t in lay.fourier_tables()]
    quad = (math.pi / lat_total) * np.sin(lay.angles)
    quad = jnp.asarray(np.concatenate([quad, quad])[None].astype(np.float32))
    mu = jnp.asarray(np.cos(lay.angles)[None].astype(np.float32))
    cuts = lay.cuts
    pair_lon = 2 * lon_local
    spectra = pl.pallas_call(
        functools.partial(forward_kernel, cuts),
        grid_spec=pltpu.PrefetchScalarGridSpec(
            num_scalar_prefetch=1,
            grid=(levels,),
            in_specs=[
                pl.BlockSpec((1, 2 * wave_total, pair_lon), lambda l, w: (w[2], 0, 0)),
                pl.BlockSpec((1,) + plane, lambda l, w: (l, 0, 0)),
                pl.BlockSpec((1,) + plane, lambda l, w: (l, 0, 0)),
                full((1, lat_total)),
            ],
            out_specs=[pl.BlockSpec((1, e - b, lat_total), lambda l, w: (l, 0, 0)) for b, e in cuts],
        ),
        out_shape=[jax.ShapeDtypeStruct((levels, e - b, lat_total), F32) for b, e in cuts],
        compiler_params=params(),
        name="forward_fourier",
    )(where, forward, folded, peer_folded, quad)

    reach = wave_total + 2 * GROUP + 2 * ROWS
    padded = jnp.concatenate([nudge_rate, jnp.zeros((2 * reach,), F32)])
    padded = lax.dynamic_slice(padded, ((place % 2) * GROUP,), (reach + GROUP,))
    by_wave = jnp.stack([padded[w : w + reach] for w in range(GROUP)], axis=1)
    rates = jnp.tile(by_wave, (1, 128 // GROUP)).reshape(reach // 2, 2, 128).transpose(1, 0, 2)

    deficits = lay.starts[1]
    scaled = tuple(
        bool(np.any(deficits[:, 128 * b : 128 * (b + 1)] > 0)) for b in range(half // 128)
    )
    buffers = [pltpu.VMEM((8 * ROWS, half), BF16)] * (4 * UNIT)
    smem = pl.BlockSpec(memory_space=pltpu.SMEM)
    plans = []
    pipeline = Pipeline(band_count)
    for q, chunk in enumerate(lay.chunks):
        items = lay.items(chunk)
        count = len(items)
        firsts = jnp.asarray(np.array([b == 0 for _, b in items], np.int32))
        locals_ = jnp.asarray(np.array([g for g, _ in items], np.int32))
        degrees = jnp.asarray(
            np.array([(2 * GROUP * chunk[g] + ROWS * max(b, 0)) // 2 for g, b in items], np.int32)
        )
        alpha, start, deficit, squares = [jnp.asarray(t) for t in lay.tables(chunk)]
        table_specs = [
            pl.BlockSpec((1, count, GROUP, 128), lambda i, w: (w[0], 0, 0, 0)),
            pl.BlockSpec((1, GROUP * len(chunk), half), lambda i, w: (w[0], 0, 0)),
            pl.BlockSpec((1, GROUP * len(chunk), half), lambda i, w: (w[0], 0, 0)),
            full((1, half)),
        ]
        rows = count // 4 * 24 * QUADS
        call = pl.pallas_call(
            functools.partial(analysis_kernel, count, levels, scaled),
            grid_spec=pltpu.PrefetchScalarGridSpec(
                num_scalar_prefetch=1,
                grid=(1,),
                in_specs=[smem, smem] + table_specs + [full(spectra[q].shape)],
                out_specs=full((4, rows, 128)),
                scratch_shapes=[pltpu.VMEM((len(chunk), 2, half, 256), BF16)] + buffers,
            ),
            out_shape=jax.ShapeDtypeStruct((4, rows, 128), F32),
            compiler_params=params(),
            cost_estimate=cost(0.5 * count),
            name="analysis",
        )
        slots = pipeline.compute(
            [spectra[q]],
            lambda spectrum: call(where, firsts, locals_, alpha, start, deficit, mu, spectrum),
        )
        pipeline.begin(q, slots)
        plans.append((count, firsts, locals_, degrees, alpha, start, deficit, squares, table_specs, rows))

    others = pipeline.compute([other_edge], lambda edge: others_call(state, edge, courant_lon, courant_lat, courant_edge))
    synths = []
    for q, plan in enumerate(plans):
        count, firsts, locals_, degrees, alpha, start, deficit, squares, table_specs, rows = plan
        while q not in pipeline.done:
            pipeline.compute([], lambda: ())
        shape = spectra[q].shape
        call = pl.pallas_call(
            functools.partial(synthesis_kernel, count, levels, scaled),
            grid_spec=pltpu.PrefetchScalarGridSpec(
                num_scalar_prefetch=1,
                grid=(1,),
                in_specs=[smem, smem, smem]
                + table_specs
                + [
                    pl.BlockSpec((1, count, ROWS, 128), lambda i, w: (w[0], 0, 0, 0)),
                    full(rates.shape),
                    full((4, rows, 128)),
                ],
                out_specs=full(shape),
                scratch_shapes=buffers,
            ),
            out_shape=jax.ShapeDtypeStruct(shape, F32),
            compiler_params=params(),
            cost_estimate=cost(0.5 * count),
            name="synthesis",
        )
        synths.append(
            pipeline.compute(
                [pipeline.done[q]],
                lambda coeffs: call(
                    where, firsts, locals_, degrees, alpha, start, deficit, mu, squares, rates, coeffs
                ),
            )
        )

    def finish(begin, share, both, theirs, whole):
        return pl.pallas_call(
            finish_kernel,
            grid=(share,),
            in_specs=[
                full((flip_width, flip_width)),
                pl.BlockSpec((1,) + plane, lambda l: (l + begin, 0, 0)),
                pl.BlockSpec((1, 1) + plane, lambda l: (0, l, 0, 0)),
                pl.BlockSpec((1,) + plane, lambda l: (l, 0, 0)),
                pl.BlockSpec(memory_space=pl.ANY),
            ],
            out_specs=pl.BlockSpec((1, 1) + plane, lambda l: (0, l + begin, 0, 0)),
            out_shape=jax.ShapeDtypeStruct(state.shape, F32),
            input_output_aliases={4: 0},
            compiler_params=params(),
            cost_estimate=cost(2.0),
            name="finish",
        )(flip, moved, both, theirs, whole)

    parts = []
    share = levels // 2 if levels % 2 == 0 else levels
    for begin in range(0, levels, share):
        both = pl.pallas_call(
            inverse_kernel,
            grid_spec=pltpu.PrefetchScalarGridSpec(
                num_scalar_prefetch=1,
                grid=(share,),
                in_specs=[pl.BlockSpec((1, 2 * pair_lon, wave_total), lambda l, w: (w[2], 0, 0))]
                + [
                    pl.BlockSpec((1, e - b, lat_total), lambda l, w, begin=begin: (l + begin, 0, 0))
                    for b, e in cuts
                ],
                out_specs=pl.BlockSpec((2, 1) + plane, lambda l, w: (0, l, 0, 0)),
            ),
            out_shape=jax.ShapeDtypeStruct((2, share) + plane, F32),
            compiler_params=params(),
            cost_estimate=cost(4.0 * share / levels),
            name="inverse_fourier",
        )(where, inverse, *synths)
        parts.append((begin, both, lax.ppermute(both[1], "band", peer)))
    whole = others
    for begin, both, theirs in parts:
        whole = finish(begin, share, both, theirs, whole)
    return whole


def solution(mesh):
    placed = (
        P("member", None, "band", None),
        P(("member", "band"), None),
        P(("member", "band"), None),
        P("member", "band", None),
        P(),
    )
    return jax.shard_map(
        body, mesh=mesh, in_specs=placed, out_specs=P("member", None, "band", None), check_vma=False
    )
```

```python
import functools
import math

import jax
import jax.numpy as jnp
import ml_dtypes
import numpy as np
from jax import lax
from jax.experimental import pallas as pl
from jax.experimental.pallas import tpu as pltpu
from jax.sharding import PartitionSpec as P

STEPS = 2
GROUP = 8
STRIPS = 8
UNIT = 2
ROWS = 64
QUADS = ROWS // 32
SHIFT = 100
DROP = 88
TOP = -12
CHUNKS = 4
F32 = jnp.float32
BF16 = jnp.bfloat16


def split_np(values):
    high = values.astype(ml_dtypes.bfloat16)
    low = (values - high.astype(np.float64)).astype(ml_dtypes.bfloat16)
    return high, low


def split(values):
    high = values.astype(BF16)
    return high, (values - high.astype(F32)).astype(BF16)


def dot(left, right):
    return jnp.dot(left, right, preferred_element_type=F32)


class Layout:
    def __init__(self, wave_total, lat_total, lon_total, band_count):
        self.waves, self.lats, self.lons, self.band = wave_total, lat_total, lon_total, band_count
        self.half = lat_total // 2
        self.groups = wave_total // (2 * GROUP)
        self.blocks = [-(-(wave_total - 2 * GROUP * t) // ROWS) for t in range(self.groups)]
        shares = [0] * CHUNKS
        self.chunks = [[] for _ in range(CHUNKS)]
        for t in sorted(range(self.groups), key=lambda t: -self.blocks[t]):
            q = int(np.argmin(shares))
            self.chunks[q].append(t)
            shares[q] += self.blocks[t]
        self.chunks = [chunk for chunk in self.chunks if chunk]
        self.order = [t for chunk in self.chunks for t in chunk]
        ends = np.cumsum([0] + [2 * GROUP * len(chunk) for chunk in self.chunks])
        self.cuts = [(int(b), int(e)) for b, e in zip(ends[:-1], ends[1:])]

    def wave_ids(self, core):
        ids = []
        for t in self.order:
            ids.append(GROUP * (2 * t + core) + np.arange(GROUP))
        return np.stack(ids)

    def items(self, chunk):
        items = [(local, b) for local, t in enumerate(chunk) for b in range(self.blocks[t])]
        while len(items) % (2 * UNIT):
            items.append((len(chunk) - 1, -1))
        return items

    @functools.cached_property
    def angles(self):
        return math.pi * (np.arange(self.half) + 0.5) / self.lats

    @functools.cached_property
    def recurrence(self):
        depth = self.waves + 2 * ROWS
        m = np.arange(self.waves, dtype=np.float64)[:, None]
        k = np.arange(depth, dtype=np.float64)[None, :]
        n = m + k
        a = np.ones((self.waves, depth))
        a[:, 1:] = np.sqrt((4 * n * n - 1)[:, 1:] / (n * n - m * m)[:, 1:])
        c = np.ones_like(a)
        c[:, 1] = a[:, 1]
        for i in range(2, depth):
            c[:, i] = a[:, i] / a[:, i - 1] * c[:, i - 2]
        alpha = np.zeros_like(a)
        alpha[:, 1:] = a[:, 1:] * c[:, :-1] / c[:, 1:]
        return alpha, c

    @functools.cached_property
    def starts(self):
        orders = np.arange(1, self.waves)
        norms = np.concatenate([[0.0], np.cumsum(np.log((2.0 * orders + 1) / (2.0 * orders)))])
        m = np.arange(self.waves)[:, None]
        logs = 0.5 * norms[:, None] + m * np.log(np.sin(self.angles))[None, :] - 0.5 * math.log(2.0)
        exps = logs / math.log(2.0) + SHIFT
        deficit = np.where(exps < -SHIFT, np.ceil((-SHIFT - exps) / DROP), 0.0)
        return np.exp2(exps + DROP * deficit), deficit

    def tables(self, chunk):
        alpha, c = self.recurrence
        mant, deficit = self.starts
        items = self.items(chunk)
        out_alpha = np.zeros((2, len(items), GROUP, 128), np.float32)
        out_c = np.zeros((2, len(items), ROWS, 128), np.float32)
        shape = (2, len(chunk) * GROUP, self.half)
        out_start, out_deficit = np.zeros(shape, np.float32), np.zeros(shape, np.float32)
        rows = np.concatenate([np.arange(0, ROWS, 2), np.arange(1, ROWS, 2)])
        for core in range(2):
            for local, t in enumerate(chunk):
                waves = GROUP * (2 * t + core) + np.arange(GROUP)
                place = slice(GROUP * local, GROUP * (local + 1))
                out_start[core, place], out_deficit[core, place] = -mant[waves], deficit[waves]
            for i, (local, b) in enumerate(items):
                if b < 0:
                    continue
                waves = GROUP * (2 * chunk[local] + core) + np.arange(GROUP)
                out_alpha[core, i, :, :ROWS] = alpha[waves, ROWS * b : ROWS * (b + 1)]
                squares = (c[waves][:, ROWS * b + rows] ** 2 * 2.0**-SHIFT).T
                squares = squares.reshape(ROWS // GROUP, GROUP, GROUP)
                for w in range(GROUP):
                    squares[:, :, w] = np.roll(squares[:, :, w], w, axis=1)
                out_c[core, i] = np.tile(squares.reshape(ROWS, GROUP), (1, 128 // GROUP))
        out_start, out_deficit = [
            t.reshape(2, -1, 2, self.half // 2).transpose(0, 2, 1, 3).reshape(4, -1, self.half // 2)
            for t in (out_start, out_deficit)
        ]
        return out_alpha, out_start, out_deficit, out_c

    def fourier_tables(self):
        local = self.lons // self.band
        forward = np.zeros((self.band, self.waves, 4 * local))
        inverse = np.zeros((self.band, 4 * local, self.waves))
        for place in range(self.band):
            waves = self.wave_ids(place % 2)
            lons = np.concatenate([local * (place ^ i) + np.arange(local) for i in (0, 2, 1, 3)])
            phase = (waves[:, :, None] * lons % self.lons) * (2 * math.pi / self.lons)
            both = np.stack([np.cos(phase), -np.sin(phase)], axis=1).reshape(self.waves, 4 * local)
            double = np.where(waves == 0, 1.0, 2.0)
            double = np.stack([double, double], axis=1).reshape(self.waves)
            forward[place] = both / self.lons
            inverse[place] = (both * double[:, None]).T
        return [np.concatenate(split_np(t), axis=1) for t in (forward, inverse)]


def south_of(cells, lane_ids):
    return jnp.where(lane_ids == 0, 0.0, pltpu.roll(cells, 1, 1))


def two_steps(cells, edge, lon, lat, lon_edge, lat_edge, store):
    shape = (8, cells.shape[1])
    row_ids = lax.broadcasted_iota(jnp.int32, shape, 0)
    lane_ids = lax.broadcasted_iota(jnp.int32, shape, 1)
    outer = jnp.broadcast_to(edge[0:1], shape)
    inner = jnp.broadcast_to(edge[1:2], shape)
    inner_once = (
        inner - lon_edge * (inner - outer) - lat_edge * (inner - south_of(inner, lane_ids))
    )

    def strip(i, carry):
        before, before_once = carry
        rows = pl.ds(pl.multiple_of(8 * i, 8), 8)
        now, east, north = cells[rows, :], lon[rows, :], lat[rows, :]
        stay = 1.0 - east - north
        turned = pltpu.roll(now, 1, 0)
        west = jnp.where(row_ids == 0, before, turned)
        once = stay * now + east * west + north * south_of(now, lane_ids)
        turned_once = pltpu.roll(once, 1, 0)
        west = jnp.where(row_ids == 0, before_once, turned_once)
        store(rows, stay * once + east * west + north * south_of(once, lane_ids))
        return turned, turned_once

    lax.fori_loop(0, cells.shape[0] // 8, strip, (inner, inner_once), unroll=STRIPS)


def reversed_lanes(values, flip):
    width = flip.shape[0]
    high, rest = split(values)
    mid = rest
    low = (values - high.astype(F32) - mid.astype(F32)).astype(BF16)
    pieces = []
    for at in range(values.shape[1] // width - 1, -1, -1):
        cut = slice(at * width, (at + 1) * width)
        pieces.append(dot(high[:, cut], flip) + (dot(mid[:, cut], flip) + dot(low[:, cut], flip)))
    return jnp.concatenate(pieces, axis=1)


def first_field_kernel(where, cells, edge, lon, lat, courant_edge, target, flip, moved, keep, send):
    def store(rows, values):
        moved[0, rows, :] = values

    two_steps(
        cells.at[0, 0], edge[0], lon, lat, courant_edge[0:1], courant_edge[1:2], store
    )
    anomaly = target[0] - moved[0]
    half = anomaly.shape[1] // 2
    north = anomaly[:, :half]
    south = reversed_lanes(anomaly[:, half:], flip[...])
    second = where[3] == 1
    for part, values in enumerate((north + south, north - south)):
        lanes = slice(part * half // 2, (part + 1) * half // 2)
        one, two = values[:, : half // 2], values[:, half // 2 :]
        keep[0, :, lanes] = jnp.where(second, two, one)
        send[0, :, lanes] = jnp.where(second, one, two)


def other_fields_kernel(cells, edge, lon, lat, courant_edge, moved):
    for p in range(cells.shape[1]):

        def store(rows, values):
            moved[0, p, rows, :] = values

        two_steps(
            cells.at[0, p], edge[p], lon, lat, courant_edge[0:1], courant_edge[1:2], store
        )


def finish_kernel(where, flip, moved, mine, theirs, far, whole, out):
    del whole
    near, far = mine[0, 0] + theirs[0], far[0]
    part = near.shape[1] // 2
    second = where[3] == 1
    ends = []
    for lanes in (slice(0, part), slice(part, 2 * part)):
        one, two = near[:, lanes], far[:, lanes]
        ends.append(
            jnp.concatenate([jnp.where(second, two, one), jnp.where(second, one, two)], axis=1)
        )
    even, odd = ends
    half = 2 * part
    out[0, 0, :, :half] = moved[0, :, :half] + (even + odd)
    out[0, 0, :, half:] = moved[0, :, half:] + reversed_lanes(even - odd, flip[...])


def forward_kernel(cuts, place, table, one, two, three, four, quad, *outs):
    del place
    a_high, a_low = split(jnp.concatenate([one[0], two[0], three[0], four[0]], axis=0))
    waves = table.shape[1] // 2
    wide = dot(table[0], a_high)
    total = (wide[:waves] + (wide[waves:] + dot(table[0, :waves], a_low))) * quad[...]
    for out, (begin, end) in zip(outs, cuts):
        out[0] = total[begin:end]


def inverse_kernel(place, table, *refs):
    del place
    out = refs[-1]
    s_high, s_low = split(jnp.concatenate([ref[0] for ref in refs[:-1]], axis=0))
    lons = table.shape[1] // 2
    wide = dot(table[0], s_high)
    total = wide[:lons] + (wide[lons:] + dot(table[0, :lons], s_low))
    for i in range(4):
        out[i, 0] = total[i * lons // 4 : (i + 1) * lons // 4]


def table_block(index, first, local, carry, alpha, start, deficit, mu, scaled, even, odd):
    earlier, latest, owed = carry
    count = len(earlier)
    fresh = first == 1
    rows = pl.ds(pl.multiple_of(local * GROUP, GROUP), GROUP)
    factors = alpha[0, index]
    earlier, latest, owed = list(earlier), list(latest), list(owed)
    for b in range(count):
        lanes = slice(128 * b, 128 * (b + 1))
        earlier[b] = jnp.where(fresh, start[0, rows, lanes], earlier[b])
        latest[b] = jnp.where(fresh, 0.0, latest[b])
        if scaled[b]:
            owed[b] = jnp.where(fresh, deficit[0, rows, lanes], owed[b])
    values = [[None] * ROWS for _ in range(count)]
    for segment in range(0, ROWS, 16):
        for b in range(count):
            if scaled[b]:
                large = jnp.abs(latest[b]) > 2.0**TOP
                down = jnp.logical_and(large, owed[b] > 0.0)
                factor = jnp.where(down, 2.0**-DROP, 1.0)
                earlier[b] = earlier[b] * factor
                latest[b] = latest[b] * factor
                owed[b] = owed[b] - jnp.where(down, 1.0, 0.0)
        for k in range(segment, segment + 16):
            spread = jnp.broadcast_to(factors[:, k : k + 1], (GROUP, 128))
            for b in range(count):
                fresh_value = (spread * mu[:, 128 * b : 128 * (b + 1)]) * latest[b] - earlier[b]
                earlier[b], latest[b] = latest[b], fresh_value
                values[b][k] = fresh_value
        for b in range(count):
            lanes = slice(128 * b, 128 * (b + 1))
            for k in range(segment, segment + 16, 4):
                for parity, store in ((0, even), (1, odd)):
                    pair = jnp.concatenate(
                        [values[b][k + parity], values[b][k + parity + 2]], axis=0
                    )
                    high, low = split(pair)
                    at = 4 * k
                    store[at : at + 16, lanes] = high
                    store[4 * ROWS + at : 4 * ROWS + at + 16, lanes] = low
        yield
    return tuple(earlier), tuple(latest), tuple(owed)


def lane_lag():
    row = lax.broadcasted_iota(jnp.int32, (GROUP, 128), 0)
    lane = lax.broadcasted_iota(jnp.int32, (GROUP, 128), 1)
    return (row + 128 - lane) % GROUP


def skewed(rows, lag):
    tile = rows[:GROUP]
    for k in range(1, GROUP):
        tile = jnp.where(lag == k, pltpu.roll(rows[GROUP * k : GROUP * (k + 1)], k, 0), tile)
    return tile


def unskewed(tile, own):
    rows = [jnp.where(own, tile, 0.0)]
    for k in range(1, GROUP):
        rows.append(jnp.where(own, pltpu.roll(tile, GROUP - k, 0), 0.0))
    return jnp.concatenate(rows, axis=0)


def run_blocks(count, tables, use, lat_blocks, scaled, sets):
    firsts, locals_, alpha, start, deficit, mu = tables
    sets = [as_pairs(ref) for ref in sets]
    angles = jnp.broadcast_to(mu[...], (GROUP, mu.shape[1]))
    zero = jnp.zeros((GROUP, 128), F32)
    carry = tuple(tuple(zero for _ in range(lat_blocks)) for _ in range(3))

    def stage(base, carry, made, used):
        using = use([jnp.maximum(base - UNIT + j, j) for j in range(UNIT)], used)

        def making(carry):
            for j in range(UNIT):
                i = base + j
                carry = yield from table_block(
                    i, firsts[i], locals_[i], carry, alpha, start, deficit, angles, scaled, *made[j]
                )
            return carry

        making = making(carry)
        pieces, segments = 2 * UNIT, UNIT * ROWS // 16
        for piece in range(pieces):
            next(using)
            for _ in range(segments // pieces):
                next(making)
        for _ in using:
            pass
        try:
            next(making)
        except StopIteration as stop:
            return stop.value

    def two(step, carry):
        for turn in range(2):
            made, used = sets[turn], sets[1 - turn]
            carry = stage(UNIT * (2 * step + turn), carry, made, used)
        return carry

    lax.fori_loop(0, count // (2 * UNIT), two, carry)
    for _ in use([jnp.int32(count - UNIT + j) for j in range(UNIT)], sets[1]):
        pass


def as_pairs(ref):
    return [(ref.at[2 * j], ref.at[2 * j + 1]) for j in range(UNIT)]


def slot_of(item, count, owned):
    quarter = item // (count // 4)
    return quarter ^ owned, (item - quarter * (count // 4)) * 24 * QUADS


def analysis_kernel(
    count,
    levels,
    scaled,
    where,
    firsts,
    locals_,
    alpha,
    start,
    deficit,
    mu,
    waves,
    keep,
    send,
    slots,
    weights,
    set_a,
    set_b,
):
    groups = waves.shape[1] // (2 * GROUP)
    half = waves.shape[2] // 2
    columns = levels * 2 * GROUP

    def prepare(group, _):
        rows = pl.ds(pl.multiple_of(group * 2 * GROUP, 2 * GROUP), 2 * GROUP)
        for parity in range(2):
            block = waves[:, rows, parity * half : (parity + 1) * half].reshape(columns, half)
            block = jnp.concatenate([block, jnp.zeros((128 - columns, half), F32)], axis=0)
            high, low = split(block.T)
            weights[group, parity, :, 0:128] = high
            weights[group, parity, :, 128:256] = low
        return 0

    lax.fori_loop(0, groups, prepare, 0)
    set_b[...] = jnp.zeros_like(set_b)
    owned = where[1]
    lag = lane_lag()
    lane = lax.broadcasted_iota(jnp.int32, (GROUP, 128), 1)
    table = 4 * ROWS

    def use(items, stores):
        for item, pair in zip(items, stores):
            sums = []
            for parity in range(2):
                both = dot(pair[parity][...], weights[locals_[item], parity])
                yield
                product = both[:table, 0:128] + (both[:table, 128:256] + both[table:, 0:128])
                sums += [skewed(product[64 * j : 64 * (j + 1)], lag) for j in range(ROWS // 16)]
            slot, at = slot_of(item, count, owned)
            for quad in range(QUADS):
                tiles = sums[4 * quad : 4 * quad + 4]
                second, third = pltpu.roll(tiles[1], 96, 1), pltpu.roll(tiles[2], 64, 1)
                packed = (
                    jnp.where(lane < 96, tiles[0], second),
                    jnp.where(lane < 64, second, third),
                    jnp.where(lane < 32, third, pltpu.roll(tiles[3], 32, 1)),
                )
                for j in range(3):
                    rows = pl.ds(pl.multiple_of(at + 24 * quad + 8 * j, 8), 8)
                    slots[slot, rows, :] = packed[j] * 2.0**-SHIFT

    run_blocks(
        count,
        (firsts, locals_, alpha, start, deficit, mu),
        use,
        half // 128,
        scaled,
        (set_a, set_b),
    )
    keep[...], send[...] = slots[0:2], slots[2:4]


def synthesis_use(
    count, levels, half, where, locals_, degrees, squares, rates, own_quarter, next_quarter,
    other_half, out, coeffs,
):
    columns = levels * 2 * GROUP
    owned = where[1]
    lane = lax.broadcasted_iota(jnp.int32, (GROUP, 128), 1)
    own = jnp.logical_and(lane_lag() == 0, lane < columns)
    out[...] = jnp.zeros_like(out)
    coeffs[0:1], coeffs[1:2], coeffs[2:4] = own_quarter[...], next_quarter[...], other_half[...]
    table = 4 * ROWS

    def use(items, stores):
        for item, pair in zip(items, stores):
            slot, at = slot_of(item, count, owned)
            tiles = []
            for quad in range(QUADS):
                packed = []
                for j in range(3):
                    rows = pl.ds(pl.multiple_of(at + 24 * quad + 8 * j, 8), 8)
                    packed.append(coeffs[slot, rows, :])
                tiles += [
                    packed[0],
                    pltpu.roll(jnp.where(lane < 64, packed[1], packed[0]), 32, 1),
                    pltpu.roll(jnp.where(lane < 32, packed[2], packed[1]), 64, 1),
                    pltpu.roll(packed[2], 96, 1),
                ]
            degree_rows = pl.ds(pl.multiple_of(degrees[item], 8), ROWS // 2)
            share = ROWS // 2
            for parity in range(2):
                parts = tiles[parity * 2 * QUADS : (parity + 1) * 2 * QUADS]
                scale = squares[0, item, share * parity : share * (parity + 1)]
                block = jnp.concatenate(parts, axis=0) * (scale * rates[parity, degree_rows])
                wide = [unskewed(block[8 * j : 8 * j + 8], own) for j in range(share // 8)]
                high, low = split(jnp.concatenate(wide, axis=0).T[:columns])
                left = jnp.concatenate(
                    [
                        jnp.concatenate([high, high], axis=1),
                        jnp.concatenate([low, jnp.zeros_like(low)], axis=1),
                    ],
                    axis=0,
                )
                total = dot(left, pair[parity][...])
                yield
                total = (total[:columns] + total[columns:]).reshape(levels, 2 * GROUP, half)
                target = pl.ds(pl.multiple_of(locals_[item] * 2 * GROUP, 2 * GROUP), 2 * GROUP)
                lanes = slice(parity * half, (parity + 1) * half)
                out[:, target, lanes] = out[:, target, lanes] + total

    return use


def synthesis_kernel(
    count,
    levels,
    scaled,
    where,
    firsts,
    locals_,
    degrees,
    alpha,
    start,
    deficit,
    mu,
    squares,
    rates,
    own_quarter,
    next_quarter,
    other_half,
    out,
    coeffs,
    set_a,
    set_b,
):
    half = mu.shape[1]
    set_b[...] = jnp.zeros_like(set_b)
    use = synthesis_use(
        count, levels, half, where, locals_, degrees, squares, rates, own_quarter, next_quarter,
        other_half, out, coeffs,
    )
    run_blocks(
        count,
        (firsts, locals_, alpha, start, deficit, mu),
        use,
        half // 128,
        scaled,
        (set_a, set_b),
    )


def chip_sum(slots, band_count):
    chips = band_count // 2
    steps = [1 << b for b in range(chips.bit_length() - 1)]
    keep, send = slots
    keep = keep + (yield send, steps[0])
    part = keep[:1] + (yield keep[1:], steps[1])
    for step in steps[2:]:
        part = part + (yield part, step)
    near = yield part, steps[1]
    return part, near, (yield jnp.concatenate([part, near], axis=0), steps[0])


def chip_move(value, step, band_count):
    ends = []
    for c in range(band_count // 2):
        ends += [(2 * c, 2 * (c ^ step)), (2 * c + 1, 2 * (c ^ step) + 1)]
    return lax.ppermute(value, "band", ends)


class Pipeline:
    def __init__(self, band_count):
        self.band_count = band_count
        self.active = {}
        self.done = {}

    def begin(self, key, slots):
        steps = chip_sum(slots, self.band_count)
        self.active[key] = [steps, next(steps)]

    def compute(self, operands, call):
        keys = list(self.active)
        payloads = [self.active[k][1][0] for k in keys]
        operands, payloads = lax.optimization_barrier((tuple(operands), payloads))
        arrived = [
            chip_move(p, self.active[k][1][1], self.band_count) for k, p in zip(keys, payloads)
        ]
        result, arrived = lax.optimization_barrier((call(*operands), arrived))
        for k, value in zip(keys, arrived):
            entry = self.active[k]
            try:
                entry[1] = entry[0].send(value)
            except StopIteration as stop:
                self.done[k] = stop.value
                del self.active[k]
        return result


def full(shape):
    return pl.BlockSpec(shape, lambda *_: (0,) * len(shape))


def cost(micros):
    return pl.CostEstimate(flops=int(micros * 1e9), bytes_accessed=1 << 20, transcendentals=0)


def params(limit=56):
    return pltpu.CompilerParams(vmem_limit_bytes=limit << 20)


def body(state, courant_lon, courant_lat, reference_field, nudge_rate):
    fields, levels, lon_local, lat_total = state.shape
    band_count = lax.axis_size("band")
    place = lax.axis_index("band")
    wave_total = nudge_rate.shape[0]
    lay = Layout(wave_total, lat_total, lon_local * band_count, band_count)
    half = lay.half
    plane = (lon_local, lat_total)
    chip = place // 2
    owned = 2 * (chip % 2) + (chip // 2) % 2
    second = chip % 2
    where = jnp.stack([place % 2, owned, place, second, 2 * (place % 2) + second]).astype(jnp.int32)

    east = [(i, (i + 1) % band_count) for i in range(band_count)]
    peer = [(i, i ^ 1) for i in range(band_count)]
    edge_rows = jnp.concatenate(
        [
            state[0, :, lon_local - STEPS :, :].reshape(levels * STEPS, lat_total),
            courant_lon[lon_local - 1 :],
            courant_lat[lon_local - 1 :],
        ],
        axis=0,
    )
    arrived = lax.ppermute(edge_rows, "band", east)
    first_edge = arrived[: levels * STEPS].reshape(levels, STEPS, lat_total)
    courant_edge = arrived[levels * STEPS :]
    flip_width = min(256, half)
    flip = jnp.asarray(np.eye(flip_width)[::-1].astype(ml_dtypes.bfloat16))

    share_lat = lat_total // 2
    strip = (lon_local, share_lat)
    moved, keep, send = pl.pallas_call(
        first_field_kernel,
        grid_spec=pltpu.PrefetchScalarGridSpec(
            num_scalar_prefetch=1,
            grid=(levels,),
            in_specs=[
                pl.BlockSpec((1, 1) + plane, lambda l, w: (0, l, 0, 0)),
                pl.BlockSpec((1, STEPS, lat_total), lambda l, w: (l, 0, 0)),
                full(plane),
                full(plane),
                full((2, lat_total)),
                pl.BlockSpec((1,) + plane, lambda l, w: (l, 0, 0)),
                full((flip_width, flip_width)),
            ],
            out_specs=[pl.BlockSpec((1,) + plane, lambda l, w: (l, 0, 0))]
            + [pl.BlockSpec((1,) + strip, lambda l, w: (l, 0, 0))] * 2,
        ),
        out_shape=[jax.ShapeDtypeStruct((levels,) + plane, F32)]
        + [jax.ShapeDtypeStruct((levels,) + strip, F32)] * 2,
        compiler_params=params(),
        name="first_field",
    )(where, state, first_edge, courant_lon, courant_lat, courant_edge, reference_field, flip)
    across = [(i, i ^ 2) for i in range(band_count)]
    peer_keep = lax.ppermute(keep, "band", peer)

    other_rows = state[1:, :, lon_local - STEPS :, :].reshape((fields - 1) * levels, STEPS, lat_total)
    other_edge = lax.ppermute(other_rows, "band", east)

    def others_call(first, last, *operands):
        def at(i):
            return (1 + first + i, 0, 0, 0)

        return pl.pallas_call(
            other_fields_kernel,
            grid=(last - first,),
            in_specs=[
                pl.BlockSpec((1, levels) + plane, at),
                pl.BlockSpec((levels, STEPS, lat_total), lambda i: (first + i, 0, 0)),
                full(plane),
                full(plane),
                full((2, lat_total)),
            ],
            out_specs=pl.BlockSpec((1, levels) + plane, at),
            out_shape=jax.ShapeDtypeStruct(state.shape, F32),
            compiler_params=params(),
            cost_estimate=cost(28.0),
            name="other_fields",
        )(*operands)

    reach = wave_total + 2 * GROUP + 2 * ROWS
    padded = jnp.concatenate([nudge_rate, jnp.zeros((2 * reach,), F32)])
    padded = lax.dynamic_slice(padded, ((place % 2) * GROUP,), (reach + GROUP,))
    by_wave = [
        jnp.roll(padded[w : w + reach].reshape(reach // 16, GROUP, 2), w, axis=1)
        for w in range(GROUP)
    ]
    by_wave = jnp.stack(by_wave, axis=-1).reshape(reach // 2, 2, GROUP).transpose(1, 0, 2)
    rates = jnp.broadcast_to(by_wave[:, :, None, :], (2, reach // 2, 128 // GROUP, GROUP))
    rates = rates.reshape(2, reach // 2, 128)

    send, other_edge = lax.optimization_barrier((send, other_edge))
    far_keep = lax.ppermute(send, "band", across)
    others = others_call(0, fields - 1, state, other_edge, courant_lon, courant_lat, courant_edge)
    others, rates, far_keep = lax.optimization_barrier((others, rates, far_keep))
    peer_far = lax.ppermute(far_keep, "band", peer)

    forward, inverse = [jnp.asarray(t) for t in lay.fourier_tables()]
    quad = (math.pi / lat_total) * np.sin(lay.angles)
    quad = np.tile(quad.reshape(2, 1, half // 2), (1, 1, 2))
    quad = jnp.asarray(quad.astype(np.float32))
    mu = jnp.asarray(np.cos(lay.angles).reshape(2, 1, half // 2).astype(np.float32))
    half = half // 2
    cuts = lay.cuts
    near_lon = 4 * lon_local
    spectra = pl.pallas_call(
        functools.partial(forward_kernel, cuts),
        grid_spec=pltpu.PrefetchScalarGridSpec(
            num_scalar_prefetch=1,
            grid=(levels,),
            in_specs=[pl.BlockSpec((1, 2 * wave_total, near_lon), lambda l, w: (w[2], 0, 0))]
            + [pl.BlockSpec((1,) + strip, lambda l, w: (l, 0, 0))] * 4
            + [pl.BlockSpec((None, 1, share_lat), lambda l, w: (w[3], 0, 0))],
            out_specs=[pl.BlockSpec((1, e - b, share_lat), lambda l, w: (l, 0, 0)) for b, e in cuts],
        ),
        out_shape=[jax.ShapeDtypeStruct((levels, e - b, share_lat), F32) for b, e in cuts],
        compiler_params=params(),
        cost_estimate=cost(8.0),
        name="forward_fourier",
    )(where, forward, keep, far_keep, peer_keep, peer_far, quad)

    deficits = lay.starts[1]
    wanted = np.any(deficits > 0, axis=0).reshape(2, half // 128, 128)
    scaled = tuple(bool(w) for w in np.any(wanted, axis=(0, 2)))
    buffers = [pltpu.VMEM((2 * UNIT, 8 * ROWS, half), BF16)] * 2
    smem = pl.BlockSpec(memory_space=pltpu.SMEM)
    plans = []
    pipeline = Pipeline(band_count)
    for q, chunk in enumerate(lay.chunks):
        items = lay.items(chunk)
        count = len(items)
        firsts = jnp.asarray(np.array([b == 0 for _, b in items], np.int32))
        locals_ = jnp.asarray(np.array([g for g, _ in items], np.int32))
        degrees = jnp.asarray(
            np.array([(2 * GROUP * chunk[g] + ROWS * max(b, 0)) // 2 for g, b in items], np.int32)
        )
        alpha, start, deficit, squares = [jnp.asarray(t) for t in lay.tables(chunk)]
        table_specs = [
            pl.BlockSpec((1, count, GROUP, 128), lambda i, w: (w[0], 0, 0, 0)),
            pl.BlockSpec((1, GROUP * len(chunk), half), lambda i, w: (w[4], 0, 0)),
            pl.BlockSpec((1, GROUP * len(chunk), half), lambda i, w: (w[4], 0, 0)),
            pl.BlockSpec((None, 1, half), lambda i, w: (w[3], 0, 0)),
        ]
        rows = count // 4 * 24 * QUADS
        call = pl.pallas_call(
            functools.partial(analysis_kernel, count, levels, scaled),
            grid_spec=pltpu.PrefetchScalarGridSpec(
                num_scalar_prefetch=1,
                grid=(1,),
                in_specs=[smem, smem] + table_specs + [full(spectra[q].shape)],
                out_specs=[full((2, rows, 128))] * 2,
                scratch_shapes=[
                    pltpu.VMEM((4, rows, 128), F32),
                    pltpu.VMEM((len(chunk), 2, half, 256), BF16),
                ]
                + buffers,
            ),
            out_shape=[jax.ShapeDtypeStruct((2, rows, 128), F32)] * 2,
            compiler_params=params(),
            cost_estimate=cost(0.5 * count),
            name="analysis",
        )
        slots = pipeline.compute(
            [spectra[q]],
            lambda spectrum: call(where, firsts, locals_, alpha, start, deficit, mu, spectrum),
        )
        pipeline.begin(q, slots)
        plans.append((count, firsts, locals_, degrees, alpha, start, deficit, squares, table_specs, rows))

    synths = []
    for q, plan in enumerate(plans):
        count, firsts, locals_, degrees, alpha, start, deficit, squares, table_specs, rows = plan
        while q not in pipeline.done:
            pipeline.compute([], lambda: ())
        shape = spectra[q].shape
        sum_specs = [
            pl.BlockSpec((1, count, ROWS, 128), lambda i, w: (w[0], 0, 0, 0)),
            full(rates.shape),
            full((1, rows, 128)),
            full((1, rows, 128)),
            full((2, rows, 128)),
        ]
        operands = [firsts, locals_, degrees, alpha, start, deficit, mu]
        call = pl.pallas_call(
            functools.partial(synthesis_kernel, count, levels, scaled),
            grid_spec=pltpu.PrefetchScalarGridSpec(
                num_scalar_prefetch=1,
                grid=(1,),
                in_specs=[smem, smem, smem] + table_specs + sum_specs,
                out_specs=full(shape),
                scratch_shapes=[pltpu.VMEM((4, rows, 128), F32)] + buffers,
            ),
            out_shape=jax.ShapeDtypeStruct(shape, F32),
            compiler_params=params(),
            cost_estimate=cost(0.5 * count),
            name="synthesis",
        )
        synths.append(
            pipeline.compute(
                pipeline.done[q],
                lambda *sums: call(where, *operands, squares, rates, *sums),
            )
        )

    def finish(begin, share, both, theirs, far, whole):
        return pl.pallas_call(
            finish_kernel,
            grid_spec=pltpu.PrefetchScalarGridSpec(
                num_scalar_prefetch=1,
                grid=(share,),
                in_specs=[
                    full((flip_width, flip_width)),
                    pl.BlockSpec((1,) + plane, lambda l, w: (l + begin, 0, 0)),
                    pl.BlockSpec((1, 1) + strip, lambda l, w: (0, l, 0, 0)),
                    pl.BlockSpec((1,) + strip, lambda l, w: (l, 0, 0)),
                    pl.BlockSpec((1,) + strip, lambda l, w: (l, 0, 0)),
                    pl.BlockSpec(memory_space=pl.ANY),
                ],
                out_specs=pl.BlockSpec((1, 1) + plane, lambda l, w: (0, l + begin, 0, 0)),
            ),
            out_shape=jax.ShapeDtypeStruct(state.shape, F32),
            input_output_aliases={6: 0},
            compiler_params=params(),
            cost_estimate=cost(2.0),
            name="finish",
        )(where, flip, moved, both, theirs, far, whole)

    parts = []
    share = levels // 2 if levels % 2 == 0 else levels
    for begin in range(0, levels, share):
        both = pl.pallas_call(
            inverse_kernel,
            grid_spec=pltpu.PrefetchScalarGridSpec(
                num_scalar_prefetch=1,
                grid=(share,),
                in_specs=[pl.BlockSpec((1, 2 * near_lon, wave_total), lambda l, w: (w[2], 0, 0))]
                + [
                    pl.BlockSpec((1, e - b, share_lat), lambda l, w, begin=begin: (l + begin, 0, 0))
                    for b, e in cuts
                ],
                out_specs=pl.BlockSpec((4, 1) + strip, lambda l, w: (0, l, 0, 0)),
            ),
            out_shape=jax.ShapeDtypeStruct((4, share) + strip, F32),
            compiler_params=params(),
            cost_estimate=cost(4.0 * share / levels),
            name="inverse_fourier",
        )(where, inverse, *synths)
        far = lax.ppermute(both[1] + lax.ppermute(both[3], "band", peer), "band", across)
        parts.append((begin, both, lax.ppermute(both[2], "band", peer), far))
    whole = others
    for begin, both, theirs, far in parts:
        whole = finish(begin, share, both, theirs, far, whole)
    return whole


def solution(mesh):
    placed = (
        P("member", None, "band", None),
        P(("member", "band"), None),
        P(("member", "band"), None),
        P("member", "band", None),
        P(),
    )
    return jax.shard_map(
        body, mesh=mesh, in_specs=placed, out_specs=P("member", None, "band", None), check_vma=False
    )
```

```python
import functools
import math

import jax
import jax.numpy as jnp
import ml_dtypes
import numpy as np
from jax import lax
from jax.experimental import pallas as pl
from jax.experimental.pallas import tpu as pltpu
from jax.sharding import PartitionSpec as P

STEPS = 2
GROUP = 8
STRIPS = 8
UNIT = 2
ROWS = 64
QUADS = ROWS // 32
SHIFT = 100
DROP = 88
TOP = -12
CHUNKS = 4
F32 = jnp.float32
BF16 = jnp.bfloat16


def split_np(values):
    high = values.astype(ml_dtypes.bfloat16)
    low = (values - high.astype(np.float64)).astype(ml_dtypes.bfloat16)
    return high, low


def split(values):
    high = values.astype(BF16)
    return high, (values - high.astype(F32)).astype(BF16)


def dot(left, right):
    return jnp.dot(left, right, preferred_element_type=F32)


class Layout:
    def __init__(self, wave_total, lat_total, lon_total, band_count):
        self.waves, self.lats, self.lons, self.band = wave_total, lat_total, lon_total, band_count
        self.half = lat_total // 2
        self.groups = wave_total // (2 * GROUP)
        self.blocks = [-(-(wave_total - 2 * GROUP * t) // ROWS) for t in range(self.groups)]
        shares = [0] * CHUNKS
        self.chunks = [[] for _ in range(CHUNKS)]
        for t in sorted(range(self.groups), key=lambda t: -self.blocks[t]):
            q = int(np.argmin(shares))
            self.chunks[q].append(t)
            shares[q] += self.blocks[t]
        self.chunks = [chunk for chunk in self.chunks if chunk]
        self.order = [t for chunk in self.chunks for t in chunk]
        ends = np.cumsum([0] + [2 * GROUP * len(chunk) for chunk in self.chunks])
        self.cuts = [(int(b), int(e)) for b, e in zip(ends[:-1], ends[1:])]

    def wave_ids(self, core):
        ids = []
        for t in self.order:
            ids.append(GROUP * (2 * t + core) + np.arange(GROUP))
        return np.stack(ids)

    def items(self, chunk):
        items = [(local, b) for local, t in enumerate(chunk) for b in range(self.blocks[t])]
        while len(items) % (2 * UNIT):
            items.append((len(chunk) - 1, -1))
        return items

    @functools.cached_property
    def angles(self):
        return math.pi * (np.arange(self.half) + 0.5) / self.lats

    @functools.cached_property
    def recurrence(self):
        depth = self.waves + 2 * ROWS
        m = np.arange(self.waves, dtype=np.float64)[:, None]
        k = np.arange(depth, dtype=np.float64)[None, :]
        n = m + k
        a = np.ones((self.waves, depth))
        a[:, 1:] = np.sqrt((4 * n * n - 1)[:, 1:] / (n * n - m * m)[:, 1:])
        c = np.ones_like(a)
        c[:, 1] = a[:, 1]
        for i in range(2, depth):
            c[:, i] = a[:, i] / a[:, i - 1] * c[:, i - 2]
        alpha = np.zeros_like(a)
        alpha[:, 1:] = a[:, 1:] * c[:, :-1] / c[:, 1:]
        return alpha, c

    @functools.cached_property
    def starts(self):
        orders = np.arange(1, self.waves)
        norms = np.concatenate([[0.0], np.cumsum(np.log((2.0 * orders + 1) / (2.0 * orders)))])
        m = np.arange(self.waves)[:, None]
        logs = 0.5 * norms[:, None] + m * np.log(np.sin(self.angles))[None, :] - 0.5 * math.log(2.0)
        exps = logs / math.log(2.0) + SHIFT
        deficit = np.where(exps < -SHIFT, np.ceil((-SHIFT - exps) / DROP), 0.0)
        return np.exp2(exps + DROP * deficit), deficit

    def tables(self, chunk):
        alpha, c = self.recurrence
        mant, deficit = self.starts
        items = self.items(chunk)
        out_alpha = np.zeros((2, len(items), GROUP, 128), np.float32)
        out_c = np.zeros((2, len(items), ROWS, 128), np.float32)
        shape = (2, len(chunk) * GROUP, self.half)
        out_start, out_deficit = np.zeros(shape, np.float32), np.zeros(shape, np.float32)
        rows = np.concatenate([np.arange(0, ROWS, 2), np.arange(1, ROWS, 2)])
        for core in range(2):
            for local, t in enumerate(chunk):
                waves = GROUP * (2 * t + core) + np.arange(GROUP)
                place = slice(GROUP * local, GROUP * (local + 1))
                out_start[core, place], out_deficit[core, place] = -mant[waves], deficit[waves]
            for i, (local, b) in enumerate(items):
                if b < 0:
                    continue
                waves = GROUP * (2 * chunk[local] + core) + np.arange(GROUP)
                out_alpha[core, i, :, :ROWS] = alpha[waves, ROWS * b : ROWS * (b + 1)]
                squares = (c[waves][:, ROWS * b + rows] ** 2 * 2.0**-SHIFT).T
                squares = squares.reshape(ROWS // GROUP, GROUP, GROUP)
                for w in range(GROUP):
                    squares[:, :, w] = np.roll(squares[:, :, w], w, axis=1)
                out_c[core, i] = np.tile(squares.reshape(ROWS, GROUP), (1, 128 // GROUP))
        out_start, out_deficit = [
            t.reshape(2, -1, 2, self.half // 2).transpose(0, 2, 1, 3).reshape(4, -1, self.half // 2)
            for t in (out_start, out_deficit)
        ]
        return out_alpha, out_start, out_deficit, out_c

    def fourier_tables(self):
        local = self.lons // self.band
        forward = np.zeros((self.band, self.waves, 4 * local))
        inverse = np.zeros((self.band, 4 * local, self.waves))
        for place in range(self.band):
            waves = self.wave_ids(place % 2)
            lons = np.concatenate([local * (place ^ i) + np.arange(local) for i in (0, 2, 1, 3)])
            phase = (waves[:, :, None] * lons % self.lons) * (2 * math.pi / self.lons)
            both = np.stack([np.cos(phase), -np.sin(phase)], axis=1).reshape(self.waves, 4 * local)
            double = np.where(waves == 0, 1.0, 2.0)
            double = np.stack([double, double], axis=1).reshape(self.waves)
            forward[place] = both / self.lons
            inverse[place] = (both * double[:, None]).T
        return [np.concatenate(split_np(t), axis=1) for t in (forward, inverse)]


def south_of(cells, lane_ids):
    return jnp.where(lane_ids == 0, 0.0, pltpu.roll(cells, 1, 1))


def two_steps(cells, edge, lon, lat, lon_edge, lat_edge, store):
    shape = (8, cells.shape[1])
    row_ids = lax.broadcasted_iota(jnp.int32, shape, 0)
    lane_ids = lax.broadcasted_iota(jnp.int32, shape, 1)
    outer = jnp.broadcast_to(edge[0:1], shape)
    inner = jnp.broadcast_to(edge[1:2], shape)
    inner_once = (
        inner - lon_edge * (inner - outer) - lat_edge * (inner - south_of(inner, lane_ids))
    )

    def strip(i, carry):
        before, before_once = carry
        rows = pl.ds(pl.multiple_of(8 * i, 8), 8)
        now, east, north = cells[rows, :], lon[rows, :], lat[rows, :]
        stay = 1.0 - east - north
        turned = pltpu.roll(now, 1, 0)
        west = jnp.where(row_ids == 0, before, turned)
        once = stay * now + east * west + north * south_of(now, lane_ids)
        turned_once = pltpu.roll(once, 1, 0)
        west = jnp.where(row_ids == 0, before_once, turned_once)
        store(rows, stay * once + east * west + north * south_of(once, lane_ids))
        return turned, turned_once

    lax.fori_loop(0, cells.shape[0] // 8, strip, (inner, inner_once), unroll=STRIPS)


def reversed_lanes(values, flip):
    width = flip.shape[0]
    high, rest = split(values)
    mid = rest
    low = (values - high.astype(F32) - mid.astype(F32)).astype(BF16)
    pieces = []
    for at in range(values.shape[1] // width - 1, -1, -1):
        cut = slice(at * width, (at + 1) * width)
        pieces.append(dot(high[:, cut], flip) + (dot(mid[:, cut], flip) + dot(low[:, cut], flip)))
    return jnp.concatenate(pieces, axis=1)


def first_field_kernel(where, cells, edge, lon, lat, courant_edge, target, flip, moved, keep, send):
    def store(rows, values):
        moved[0, rows, :] = values

    two_steps(
        cells.at[0, 0], edge[0], lon, lat, courant_edge[0:1], courant_edge[1:2], store
    )
    anomaly = target[0] - moved[0]
    half = anomaly.shape[1] // 2
    north = anomaly[:, :half]
    south = reversed_lanes(anomaly[:, half:], flip[...])
    second = where[3] == 1
    for part, values in enumerate((north + south, north - south)):
        lanes = slice(part * half // 2, (part + 1) * half // 2)
        one, two = values[:, : half // 2], values[:, half // 2 :]
        keep[0, :, lanes] = jnp.where(second, two, one)
        send[0, :, lanes] = jnp.where(second, one, two)


def other_fields_kernel(cells, edge, lon, lat, courant_edge, moved):
    for p in range(cells.shape[1]):

        def store(rows, values):
            moved[0, p, rows, :] = values

        two_steps(
            cells.at[0, p], edge[p], lon, lat, courant_edge[0:1], courant_edge[1:2], store
        )


def finish_kernel(where, flip, moved, mine, theirs, far, whole, out):
    del whole
    near, far = mine[0, 0] + theirs[0], far[0]
    part = near.shape[1] // 2
    second = where[3] == 1
    ends = []
    for lanes in (slice(0, part), slice(part, 2 * part)):
        one, two = near[:, lanes], far[:, lanes]
        ends.append(
            jnp.concatenate([jnp.where(second, two, one), jnp.where(second, one, two)], axis=1)
        )
    even, odd = ends
    half = 2 * part
    out[0, 0, :, :half] = moved[0, :, :half] + (even + odd)
    out[0, 0, :, half:] = moved[0, :, half:] + reversed_lanes(even - odd, flip[...])


def forward_kernel(cuts, place, table, one, two, three, four, quad, *outs):
    del place
    a_high, a_low = split(jnp.concatenate([one[0], two[0], three[0], four[0]], axis=0))
    waves = table.shape[1] // 2
    wide = dot(table[0], a_high)
    total = (wide[:waves] + (wide[waves:] + dot(table[0, :waves], a_low))) * quad[...]
    for out, (begin, end) in zip(outs, cuts):
        out[0] = total[begin:end]


def inverse_kernel(place, table, *refs):
    del place
    out = refs[-1]
    s_high, s_low = split(jnp.concatenate([ref[0] for ref in refs[:-1]], axis=0))
    lons = table.shape[1] // 2
    wide = dot(table[0], s_high)
    total = wide[:lons] + (wide[lons:] + dot(table[0, :lons], s_low))
    for i in range(4):
        out[i, 0] = total[i * lons // 4 : (i + 1) * lons // 4]


def table_block(index, first, local, carry, alpha, start, deficit, mu, scaled, even, odd):
    earlier, latest, owed = carry
    count = len(earlier)
    fresh = first == 1
    rows = pl.ds(pl.multiple_of(local * GROUP, GROUP), GROUP)
    factors = alpha[0, index]
    earlier, latest, owed = list(earlier), list(latest), list(owed)
    for b in range(count):
        lanes = slice(128 * b, 128 * (b + 1))
        earlier[b] = jnp.where(fresh, start[0, rows, lanes], earlier[b])
        latest[b] = jnp.where(fresh, 0.0, latest[b])
        if scaled[b]:
            owed[b] = jnp.where(fresh, deficit[0, rows, lanes], owed[b])
    values = [[None] * ROWS for _ in range(count)]
    for segment in range(0, ROWS, 16):
        for b in range(count):
            if scaled[b]:
                large = jnp.abs(latest[b]) > 2.0**TOP
                down = jnp.logical_and(large, owed[b] > 0.0)
                factor = jnp.where(down, 2.0**-DROP, 1.0)
                earlier[b] = earlier[b] * factor
                latest[b] = latest[b] * factor
                owed[b] = owed[b] - jnp.where(down, 1.0, 0.0)
        for k in range(segment, segment + 16):
            spread = jnp.broadcast_to(factors[:, k : k + 1], (GROUP, 128))
            for b in range(count):
                fresh_value = (spread * mu[:, 128 * b : 128 * (b + 1)]) * latest[b] - earlier[b]
                earlier[b], latest[b] = latest[b], fresh_value
                values[b][k] = fresh_value
        for b in range(count):
            lanes = slice(128 * b, 128 * (b + 1))
            for k in range(segment, segment + 16, 4):
                for parity, store in ((0, even), (1, odd)):
                    pair = jnp.concatenate(
                        [values[b][k + parity], values[b][k + parity + 2]], axis=0
                    )
                    high, low = split(pair)
                    at = 4 * k
                    store[at : at + 16, lanes] = high
                    store[4 * ROWS + at : 4 * ROWS + at + 16, lanes] = low
        yield
    return tuple(earlier), tuple(latest), tuple(owed)


def lane_lag():
    row = lax.broadcasted_iota(jnp.int32, (GROUP, 128), 0)
    lane = lax.broadcasted_iota(jnp.int32, (GROUP, 128), 1)
    return (row + 128 - lane) % GROUP


def skewed(rows, lag):
    tile = rows[:GROUP]
    for k in range(1, GROUP):
        tile = jnp.where(lag == k, pltpu.roll(rows[GROUP * k : GROUP * (k + 1)], k, 0), tile)
    return tile


def unskewed(tile, own):
    rows = [jnp.where(own, tile, 0.0)]
    for k in range(1, GROUP):
        rows.append(jnp.where(own, pltpu.roll(tile, GROUP - k, 0), 0.0))
    return jnp.concatenate(rows, axis=0)


def run_blocks(count, tables, use, lat_blocks, scaled, sets):
    firsts, locals_, alpha, start, deficit, mu = tables
    sets = [as_pairs(ref) for ref in sets]
    angles = jnp.broadcast_to(mu[...], (GROUP, mu.shape[1]))
    zero = jnp.zeros((GROUP, 128), F32)
    carry = tuple(tuple(zero for _ in range(lat_blocks)) for _ in range(3))

    def stage(base, carry, made, used):
        using = use([jnp.maximum(base - UNIT + j, j) for j in range(UNIT)], used)

        def making(carry):
            for j in range(UNIT):
                i = base + j
                carry = yield from table_block(
                    i, firsts[i], locals_[i], carry, alpha, start, deficit, angles, scaled, *made[j]
                )
            return carry

        making = making(carry)
        pieces, segments = 2 * UNIT, UNIT * ROWS // 16
        for piece in range(pieces):
            next(using)
            for _ in range(segments // pieces):
                next(making)
        for _ in using:
            pass
        try:
            next(making)
        except StopIteration as stop:
            return stop.value

    def two(step, carry):
        for turn in range(2):
            made, used = sets[turn], sets[1 - turn]
            carry = stage(UNIT * (2 * step + turn), carry, made, used)
        return carry

    lax.fori_loop(0, count // (2 * UNIT), two, carry)
    for _ in use([jnp.int32(count - UNIT + j) for j in range(UNIT)], sets[1]):
        pass


def as_pairs(ref):
    return [(ref.at[2 * j], ref.at[2 * j + 1]) for j in range(UNIT)]


def slot_of(item, count, owned):
    quarter = item // (count // 4)
    return quarter ^ owned, (item - quarter * (count // 4)) * 24 * QUADS


def analysis_kernel(
    count,
    levels,
    scaled,
    where,
    firsts,
    locals_,
    alpha,
    start,
    deficit,
    mu,
    waves,
    keep,
    send,
    slots,
    weights,
    set_a,
    set_b,
):
    groups = waves.shape[1] // (2 * GROUP)
    half = waves.shape[2] // 2
    columns = levels * 2 * GROUP

    def prepare(group, _):
        rows = pl.ds(pl.multiple_of(group * 2 * GROUP, 2 * GROUP), 2 * GROUP)
        for parity in range(2):
            block = waves[:, rows, parity * half : (parity + 1) * half].reshape(columns, half)
            block = jnp.concatenate([block, jnp.zeros((128 - columns, half), F32)], axis=0)
            high, low = split(block.T)
            weights[group, parity, :, 0:128] = high
            weights[group, parity, :, 128:256] = low
        return 0

    lax.fori_loop(0, groups, prepare, 0)
    set_b[...] = jnp.zeros_like(set_b)
    owned = where[1]
    lag = lane_lag()
    lane = lax.broadcasted_iota(jnp.int32, (GROUP, 128), 1)
    table = 4 * ROWS

    def use(items, stores):
        for item, pair in zip(items, stores):
            sums = []
            for parity in range(2):
                both = dot(pair[parity][...], weights[locals_[item], parity])
                yield
                product = both[:table, 0:128] + (both[:table, 128:256] + both[table:, 0:128])
                sums += [skewed(product[64 * j : 64 * (j + 1)], lag) for j in range(ROWS // 16)]
            slot, at = slot_of(item, count, owned)
            for quad in range(QUADS):
                tiles = sums[4 * quad : 4 * quad + 4]
                second, third = pltpu.roll(tiles[1], 96, 1), pltpu.roll(tiles[2], 64, 1)
                packed = (
                    jnp.where(lane < 96, tiles[0], second),
                    jnp.where(lane < 64, second, third),
                    jnp.where(lane < 32, third, pltpu.roll(tiles[3], 32, 1)),
                )
                for j in range(3):
                    rows = pl.ds(pl.multiple_of(at + 24 * quad + 8 * j, 8), 8)
                    slots[slot, rows, :] = packed[j] * 2.0**-SHIFT

    run_blocks(
        count,
        (firsts, locals_, alpha, start, deficit, mu),
        use,
        half // 128,
        scaled,
        (set_a, set_b),
    )
    keep[...], send[...] = slots[0:2], slots[2:4]


def synthesis_use(
    count, levels, half, where, locals_, degrees, squares, rates, own_quarter, next_quarter,
    other_half, out, coeffs,
):
    columns = levels * 2 * GROUP
    owned = where[1]
    lane = lax.broadcasted_iota(jnp.int32, (GROUP, 128), 1)
    own = jnp.logical_and(lane_lag() == 0, lane < columns)
    out[...] = jnp.zeros_like(out)
    coeffs[0:1], coeffs[1:2], coeffs[2:4] = own_quarter[...], next_quarter[...], other_half[...]
    table = 4 * ROWS

    def use(items, stores):
        for item, pair in zip(items, stores):
            slot, at = slot_of(item, count, owned)
            tiles = []
            for quad in range(QUADS):
                packed = []
                for j in range(3):
                    rows = pl.ds(pl.multiple_of(at + 24 * quad + 8 * j, 8), 8)
                    packed.append(coeffs[slot, rows, :])
                tiles += [
                    packed[0],
                    pltpu.roll(jnp.where(lane < 64, packed[1], packed[0]), 32, 1),
                    pltpu.roll(jnp.where(lane < 32, packed[2], packed[1]), 64, 1),
                    pltpu.roll(packed[2], 96, 1),
                ]
            degree_rows = pl.ds(pl.multiple_of(degrees[item], 8), ROWS // 2)
            share = ROWS // 2
            for parity in range(2):
                parts = tiles[parity * 2 * QUADS : (parity + 1) * 2 * QUADS]
                scale = squares[0, item, share * parity : share * (parity + 1)]
                block = jnp.concatenate(parts, axis=0) * (scale * rates[parity, degree_rows])
                wide = [unskewed(block[8 * j : 8 * j + 8], own) for j in range(share // 8)]
                high, low = split(jnp.concatenate(wide, axis=0).T[:columns])
                left = jnp.concatenate(
                    [
                        jnp.concatenate([high, high], axis=1),
                        jnp.concatenate([low, jnp.zeros_like(low)], axis=1),
                    ],
                    axis=0,
                )
                total = dot(left, pair[parity][...])
                yield
                total = (total[:columns] + total[columns:]).reshape(levels, 2 * GROUP, half)
                target = pl.ds(pl.multiple_of(locals_[item] * 2 * GROUP, 2 * GROUP), 2 * GROUP)
                lanes = slice(parity * half, (parity + 1) * half)
                out[:, target, lanes] = out[:, target, lanes] + total

    return use


def synthesis_kernel(
    count,
    levels,
    scaled,
    where,
    firsts,
    locals_,
    degrees,
    alpha,
    start,
    deficit,
    mu,
    squares,
    rates,
    own_quarter,
    next_quarter,
    other_half,
    out,
    coeffs,
    set_a,
    set_b,
):
    half = mu.shape[1]
    set_b[...] = jnp.zeros_like(set_b)
    use = synthesis_use(
        count, levels, half, where, locals_, degrees, squares, rates, own_quarter, next_quarter,
        other_half, out, coeffs,
    )
    run_blocks(
        count,
        (firsts, locals_, alpha, start, deficit, mu),
        use,
        half // 128,
        scaled,
        (set_a, set_b),
    )


def chip_sum(slots, band_count):
    chips = band_count // 2
    steps = [1 << b for b in range(chips.bit_length() - 1)]
    keep, send = slots
    keep = keep + (yield send, steps[0])
    part = keep[:1] + (yield keep[1:], steps[1])
    for step in steps[2:]:
        part = part + (yield part, step)
    near = yield part, steps[1]
    return part, near, (yield jnp.concatenate([part, near], axis=0), steps[0])


def chip_move(value, step, band_count):
    ends = []
    for c in range(band_count // 2):
        ends += [(2 * c, 2 * (c ^ step)), (2 * c + 1, 2 * (c ^ step) + 1)]
    return lax.ppermute(value, "band", ends)


class Pipeline:
    def __init__(self, band_count):
        self.band_count = band_count
        self.active = {}
        self.done = {}

    def begin(self, key, slots):
        steps = chip_sum(slots, self.band_count)
        self.active[key] = [steps, next(steps)]

    def compute(self, operands, call):
        keys = list(self.active)
        payloads = [self.active[k][1][0] for k in keys]
        operands, payloads = lax.optimization_barrier((tuple(operands), payloads))
        arrived = [
            chip_move(p, self.active[k][1][1], self.band_count) for k, p in zip(keys, payloads)
        ]
        result, arrived = lax.optimization_barrier((call(*operands), arrived))
        for k, value in zip(keys, arrived):
            entry = self.active[k]
            try:
                entry[1] = entry[0].send(value)
            except StopIteration as stop:
                self.done[k] = stop.value
                del self.active[k]
        return result


def full(shape):
    return pl.BlockSpec(shape, lambda *_: (0,) * len(shape))


def cost(micros):
    return pl.CostEstimate(flops=int(micros * 1e9), bytes_accessed=1 << 20, transcendentals=0)


def params(limit):
    return pltpu.CompilerParams(vmem_limit_bytes=limit << 20)


def body(state, courant_lon, courant_lat, reference_field, nudge_rate):
    fields, levels, lon_local, lat_total = state.shape
    band_count = lax.axis_size("band")
    place = lax.axis_index("band")
    wave_total = nudge_rate.shape[0]
    lay = Layout(wave_total, lat_total, lon_local * band_count, band_count)
    half = lay.half
    plane = (lon_local, lat_total)
    chip = place // 2
    owned = 2 * (chip % 2) + (chip // 2) % 2
    second = chip % 2
    where = jnp.stack([place % 2, owned, place, second, 2 * (place % 2) + second]).astype(jnp.int32)

    east = [(i, (i + 1) % band_count) for i in range(band_count)]
    peer = [(i, i ^ 1) for i in range(band_count)]
    edge_rows = jnp.concatenate(
        [
            state[0, :, lon_local - STEPS :, :].reshape(levels * STEPS, lat_total),
            courant_lon[lon_local - 1 :],
            courant_lat[lon_local - 1 :],
        ],
        axis=0,
    )
    arrived = lax.ppermute(edge_rows, "band", east)
    first_edge = arrived[: levels * STEPS].reshape(levels, STEPS, lat_total)
    courant_edge = arrived[levels * STEPS :]
    flip_width = min(256, half)
    flip = jnp.asarray(np.eye(flip_width)[::-1].astype(ml_dtypes.bfloat16))

    share_lat = lat_total // 2
    strip = (lon_local, share_lat)
    moved, keep, send = pl.pallas_call(
        first_field_kernel,
        grid_spec=pltpu.PrefetchScalarGridSpec(
            num_scalar_prefetch=1,
            grid=(levels,),
            in_specs=[
                pl.BlockSpec((1, 1) + plane, lambda l, w: (0, l, 0, 0)),
                pl.BlockSpec((1, STEPS, lat_total), lambda l, w: (l, 0, 0)),
                full(plane),
                full(plane),
                full((2, lat_total)),
                pl.BlockSpec((1,) + plane, lambda l, w: (l, 0, 0)),
                full((flip_width, flip_width)),
            ],
            out_specs=[pl.BlockSpec((1,) + plane, lambda l, w: (l, 0, 0))]
            + [pl.BlockSpec((1,) + strip, lambda l, w: (l, 0, 0))] * 2,
        ),
        out_shape=[jax.ShapeDtypeStruct((levels,) + plane, F32)]
        + [jax.ShapeDtypeStruct((levels,) + strip, F32)] * 2,
        compiler_params=params(56),
        name="first_field",
    )(where, state, first_edge, courant_lon, courant_lat, courant_edge, reference_field, flip)
    across = [(i, i ^ 2) for i in range(band_count)]
    peer_keep = lax.ppermute(keep, "band", peer)

    other_rows = state[1:, :, lon_local - STEPS :, :].reshape((fields - 1) * levels, STEPS, lat_total)
    other_edge = lax.ppermute(other_rows, "band", east)

    def others_call(first, last, *operands):
        def at(i):
            return (1 + first + i, 0, 0, 0)

        return pl.pallas_call(
            other_fields_kernel,
            grid=(last - first,),
            in_specs=[
                pl.BlockSpec((1, levels) + plane, at),
                pl.BlockSpec((levels, STEPS, lat_total), lambda i: (first + i, 0, 0)),
                full(plane),
                full(plane),
                full((2, lat_total)),
            ],
            out_specs=pl.BlockSpec((1, levels) + plane, at),
            out_shape=jax.ShapeDtypeStruct(state.shape, F32),
            compiler_params=params(56),
            cost_estimate=cost(28.0),
            name="other_fields",
        )(*operands)

    reach = wave_total + 2 * GROUP + 2 * ROWS
    padded = jnp.concatenate([nudge_rate, jnp.zeros((2 * reach,), F32)])
    padded = lax.dynamic_slice(padded, ((place % 2) * GROUP,), (reach + GROUP,))
    by_wave = [
        jnp.roll(padded[w : w + reach].reshape(reach // 16, GROUP, 2), w, axis=1)
        for w in range(GROUP)
    ]
    by_wave = jnp.stack(by_wave, axis=-1).reshape(reach // 2, 2, GROUP).transpose(1, 0, 2)
    rates = jnp.broadcast_to(by_wave[:, :, None, :], (2, reach // 2, 128 // GROUP, GROUP))
    rates = rates.reshape(2, reach // 2, 128)

    send, other_edge = lax.optimization_barrier((send, other_edge))
    far_keep = lax.ppermute(send, "band", across)
    others = others_call(0, fields - 1, state, other_edge, courant_lon, courant_lat, courant_edge)
    others, rates, far_keep = lax.optimization_barrier((others, rates, far_keep))
    peer_far = lax.ppermute(far_keep, "band", peer)

    forward, inverse = [jnp.asarray(t) for t in lay.fourier_tables()]
    quad = (math.pi / lat_total) * np.sin(lay.angles)
    quad = np.tile(quad.reshape(2, 1, half // 2), (1, 1, 2))
    quad = jnp.asarray(quad.astype(np.float32))
    mu = jnp.asarray(np.cos(lay.angles).reshape(2, 1, half // 2).astype(np.float32))
    half = half // 2
    cuts = lay.cuts
    near_lon = 4 * lon_local
    spectra = pl.pallas_call(
        functools.partial(forward_kernel, cuts),
        grid_spec=pltpu.PrefetchScalarGridSpec(
            num_scalar_prefetch=1,
            grid=(levels,),
            in_specs=[pl.BlockSpec((1, 2 * wave_total, near_lon), lambda l, w: (w[2], 0, 0))]
            + [pl.BlockSpec((1,) + strip, lambda l, w: (l, 0, 0))] * 4
            + [pl.BlockSpec((None, 1, share_lat), lambda l, w: (w[3], 0, 0))],
            out_specs=[pl.BlockSpec((1, e - b, share_lat), lambda l, w: (l, 0, 0)) for b, e in cuts],
        ),
        out_shape=[jax.ShapeDtypeStruct((levels, e - b, share_lat), F32) for b, e in cuts],
        compiler_params=params(20),
        cost_estimate=cost(8.0),
        name="forward_fourier",
    )(where, forward, keep, far_keep, peer_keep, peer_far, quad)

    deficits = lay.starts[1]
    wanted = np.any(deficits > 0, axis=0).reshape(2, half // 128, 128)
    scaled = tuple(bool(w) for w in np.any(wanted, axis=(0, 2)))
    buffers = [pltpu.VMEM((2 * UNIT, 8 * ROWS, half), BF16)] * 2
    smem = pl.BlockSpec(memory_space=pltpu.SMEM)
    plans = []
    pipeline = Pipeline(band_count)
    for q, chunk in enumerate(lay.chunks):
        items = lay.items(chunk)
        count = len(items)
        firsts = jnp.asarray(np.array([b == 0 for _, b in items], np.int32))
        locals_ = jnp.asarray(np.array([g for g, _ in items], np.int32))
        degrees = jnp.asarray(
            np.array([(2 * GROUP * chunk[g] + ROWS * max(b, 0)) // 2 for g, b in items], np.int32)
        )
        alpha, start, deficit, squares = [jnp.asarray(t) for t in lay.tables(chunk)]
        table_specs = [
            pl.BlockSpec((1, count, GROUP, 128), lambda i, w: (w[0], 0, 0, 0)),
            pl.BlockSpec((1, GROUP * len(chunk), half), lambda i, w: (w[4], 0, 0)),
            pl.BlockSpec((1, GROUP * len(chunk), half), lambda i, w: (w[4], 0, 0)),
            pl.BlockSpec((None, 1, half), lambda i, w: (w[3], 0, 0)),
        ]
        rows = count // 4 * 24 * QUADS
        call = pl.pallas_call(
            functools.partial(analysis_kernel, count, levels, scaled),
            grid_spec=pltpu.PrefetchScalarGridSpec(
                num_scalar_prefetch=1,
                grid=(1,),
                in_specs=[smem, smem] + table_specs + [full(spectra[q].shape)],
                out_specs=[full((2, rows, 128))] * 2,
                scratch_shapes=[
                    pltpu.VMEM((4, rows, 128), F32),
                    pltpu.VMEM((len(chunk), 2, half, 256), BF16),
                ]
                + buffers,
            ),
            out_shape=[jax.ShapeDtypeStruct((2, rows, 128), F32)] * 2,
            compiler_params=params(20),
            cost_estimate=cost(0.5 * count),
            name="analysis",
        )
        slots = pipeline.compute(
            [spectra[q]],
            lambda spectrum: call(where, firsts, locals_, alpha, start, deficit, mu, spectrum),
        )
        pipeline.begin(q, slots)
        plans.append((count, firsts, locals_, degrees, alpha, start, deficit, squares, table_specs, rows))

    synths = []
    for q, plan in enumerate(plans):
        count, firsts, locals_, degrees, alpha, start, deficit, squares, table_specs, rows = plan
        while q not in pipeline.done:
            pipeline.compute([], lambda: ())
        shape = spectra[q].shape
        sum_specs = [
            pl.BlockSpec((1, count, ROWS, 128), lambda i, w: (w[0], 0, 0, 0)),
            full(rates.shape),
            full((1, rows, 128)),
            full((1, rows, 128)),
            full((2, rows, 128)),
        ]
        operands = [firsts, locals_, degrees, alpha, start, deficit, mu]
        call = pl.pallas_call(
            functools.partial(synthesis_kernel, count, levels, scaled),
            grid_spec=pltpu.PrefetchScalarGridSpec(
                num_scalar_prefetch=1,
                grid=(1,),
                in_specs=[smem, smem, smem] + table_specs + sum_specs,
                out_specs=full(shape),
                scratch_shapes=[pltpu.VMEM((4, rows, 128), F32)] + buffers,
            ),
            out_shape=jax.ShapeDtypeStruct(shape, F32),
            compiler_params=params(20),
            cost_estimate=cost(0.5 * count),
            name="synthesis",
        )
        synths.append(
            pipeline.compute(
                pipeline.done[q],
                lambda *sums: call(where, *operands, squares, rates, *sums),
            )
        )

    def finish(begin, share, both, theirs, far, whole):
        return pl.pallas_call(
            finish_kernel,
            grid_spec=pltpu.PrefetchScalarGridSpec(
                num_scalar_prefetch=1,
                grid=(share,),
                in_specs=[
                    full((flip_width, flip_width)),
                    pl.BlockSpec((1,) + plane, lambda l, w: (l + begin, 0, 0)),
                    pl.BlockSpec((1, 1) + strip, lambda l, w: (0, l, 0, 0)),
                    pl.BlockSpec((1,) + strip, lambda l, w: (l, 0, 0)),
                    pl.BlockSpec((1,) + strip, lambda l, w: (l, 0, 0)),
                    pl.BlockSpec(memory_space=pl.ANY),
                ],
                out_specs=pl.BlockSpec((1, 1) + plane, lambda l, w: (0, l + begin, 0, 0)),
            ),
            out_shape=jax.ShapeDtypeStruct(state.shape, F32),
            input_output_aliases={6: 0},
            compiler_params=params(20),
            cost_estimate=cost(2.0),
            name="finish",
        )(where, flip, moved, both, theirs, far, whole)

    parts = []
    share = levels // 2 if levels % 2 == 0 else levels
    for begin in range(0, levels, share):
        both = pl.pallas_call(
            inverse_kernel,
            grid_spec=pltpu.PrefetchScalarGridSpec(
                num_scalar_prefetch=1,
                grid=(share,),
                in_specs=[pl.BlockSpec((1, 2 * near_lon, wave_total), lambda l, w: (w[2], 0, 0))]
                + [
                    pl.BlockSpec((1, e - b, share_lat), lambda l, w, begin=begin: (l + begin, 0, 0))
                    for b, e in cuts
                ],
                out_specs=pl.BlockSpec((4, 1) + strip, lambda l, w: (0, l, 0, 0)),
            ),
            out_shape=jax.ShapeDtypeStruct((4, share) + strip, F32),
            compiler_params=params(20),
            cost_estimate=cost(4.0 * share / levels),
            name="inverse_fourier",
        )(where, inverse, *synths)
        far = lax.ppermute(both[1] + lax.ppermute(both[3], "band", peer), "band", across)
        parts.append((begin, both, lax.ppermute(both[2], "band", peer), far))
    whole = others
    for begin, both, theirs, far in parts:
        whole = finish(begin, share, both, theirs, far, whole)
    return whole


def solution(mesh):
    placed = (
        P("member", None, "band", None),
        P(("member", "band"), None),
        P(("member", "band"), None),
        P("member", "band", None),
        P(),
    )
    return jax.shard_map(
        body, mesh=mesh, in_specs=placed, out_specs=P("member", None, "band", None), check_vma=False
    )
```
